32 devices in a mesh: gx: 8 (over z, x), gy: 4 (over y, core).
Axes of the slice: x: 2, y: 2, z: 4, core: 2. Of those that a mesh axis runs over, the one named last changes fastest.
Arguments:
- source: float32 [6, 64, 64, 128], P(None, 'gx', 'gy'), may hold values from -6 to 6
- cell_class: int32 [64, 64, 128], P('gx', 'gy'), may hold values from 0 to 7
- class_conductivity: float32 [8], replicated, may hold values from 0.1 to 3
- layer_of_depth: int32 [64], replicated, may hold values from 0 to 7
- inverses: float32 [8, 192, 192], replicated, as said below
Outputs:
- correction: float32 [6, 64, 64, 128], P(None, 'gx', 'gy')
The draws below stay inside these ranges and needn't reach their ends.
Inputs may be any that keep to these rules, and one draw needn't show every extreme that they name: `inverses`: each matrix has a positive diagonal.
All inputs are finite; a program needn't handle non-finite values.
Results may differ from the reference program's by a relative error of at most 0.000054.
Values sent between devices are 32-bit elements; how exact they have to be, the bound alone decides.
A program may use at most 128 MiB of HBM per device.

```python
import math
import jax
import jax.numpy as jnp
from jax import lax

CZ = 128
BLOCK = 192
NLAYER = 8
NCLASS = 8
NX = 64
NY = 64
NZB = 64


def draw_inverses(key, part):
    key_diag, key_off = jax.random.split(key, 2)
    diag = jax.random.uniform(key_diag, (NLAYER, BLOCK), jnp.float32, 0.12, 0.2)
    off = jax.random.normal(key_off, (NLAYER, BLOCK, BLOCK), jnp.float32) * 0.008
    eye = jnp.eye(BLOCK, dtype=jnp.float32)
    return off * (1.0 - eye[None]) + eye[None] * diag[:, :, None]


def set_ends(values, own_key, low, high):
    place = [jax.random.randint(jax.random.fold_in(own_key, axis), (), 0, length) for axis, length in enumerate(values.shape)]
    longest = values.shape.index(max(values.shape))
    neighbour = place[:longest] + [(place[longest] + 1) % values.shape[longest]] + place[longest + 1:]
    return values.at[tuple(place)].set(low).at[tuple(neighbour)].set(high)


def level_of(own_key, extent, cuts, smallest, high):
    factor_of = 1.0
    for axis_at, parts in cuts:
        draws = jax.random.uniform(jax.random.fold_in(jax.random.fold_in(own_key, 6), axis_at), (parts,), jnp.float32, smallest / len(cuts), high / len(cuts))
        factor_of = factor_of * jnp.repeat(jnp.exp(draws), extent[axis_at] // parts).reshape((-1,) + (1,) * (len(extent) - 1 - axis_at))
    return factor_of


def gaussian(key, dims, spread, reach, pieces=(), kind=jnp.bfloat16):
    array = jax.random.normal(key, dims, jnp.float32) * spread
    if len(pieces) > 0:
        array = level_of(key, dims, pieces, -0.22, 0.18) * array
    return jnp.clip(array, min=-reach, max=reach).astype(kind)


def setup_inputs(seed: int = 0) -> dict:
    key_list = jax.random.split(jax.random.key(seed), 6)
    source = gaussian(key_list[0], (6, NX, NY, CZ), 1.0, 6.0, ((1, 8), (2, 4)), jnp.float32)
    cell_class = set_ends(jax.random.randint(key_list[1], (NX, NY, CZ), 0, NCLASS), jax.random.fold_in(key_list[1], 1), 0, NCLASS - 1).astype(jnp.int32)
    class_conductivity = jnp.clip(jnp.exp(jax.random.uniform(key_list[2], (NCLASS,), jnp.float32, math.log(0.1), math.log(3.0))), 0.1, 3.0)
    layer_of_depth = set_ends(jax.random.randint(key_list[3], (NZB,), 0, NLAYER), jax.random.fold_in(key_list[3], 1), 0, NLAYER - 1).astype(jnp.int32)
    inverses = draw_inverses(jax.random.fold_in(key_list[5], 71), 0)
    return {"source": source, "cell_class": cell_class, "class_conductivity": class_conductivity, "layer_of_depth": layer_of_depth, "inverses": inverses}


damping = 0.8


def apply_operator(field, sigma, level):
    padded = jnp.pad(field, ((0, 0), (1, 1), (1, 1), (1, 1)))
    beside = padded[:, 2:, 1:-1, 1:-1] + padded[:, :-2, 1:-1, 1:-1]
    beside = beside + padded[:, 1:-1, 2:, 1:-1] + padded[:, 1:-1, :-2, 1:-1]
    beside = beside + padded[:, 1:-1, 1:-1, 2:] + padded[:, 1:-1, 1:-1, :-2]
    lapl = (6.0 * field - beside) / (4.0 ** level)
    real_part = lapl[:3] - sigma[None] * field[3:]
    imag_part = lapl[3:] + sigma[None] * field[:3]
    return jnp.concatenate([real_part, imag_part], axis=0)


def to_blocks(field):
    comps, sx, sy, sz = field.shape
    shaped = field.reshape(comps, sx // 4, 4, sy // 4, 4, sz // 2, 2)
    return shaped.transpose(5, 1, 3, 0, 2, 4, 6).reshape(sz // 2, (sx // 4) * (sy // 4), comps * 32)


def from_blocks(blocks, comps, sx, sy, sz):
    shaped = blocks.reshape(sz // 2, sx // 4, sy // 4, comps, 4, 4, 2)
    return shaped.transpose(3, 1, 4, 2, 5, 0, 6).reshape(comps, sx, sy, sz)


def smooth(field, inverses, layer_ids, level):
    comps, sx, sy, sz = field.shape
    blocks = to_blocks(field)
    matrices = jnp.take(inverses, layer_ids.astype(jnp.int32), axis=0)
    total = jnp.einsum("zrk,zjk->zrj", blocks, matrices, precision=lax.Precision.HIGHEST)
    total = total * (damping * 4.0 ** level)
    return from_blocks(total, comps, sx, sy, sz)


def restrict(field):
    sx, sy, sz = field.shape[-3:]
    shaped = field.reshape(field.shape[:-3] + (sx // 2, 2, sy // 2, 2, sz // 2, 2))
    return shaped.mean(axis=(-5, -3, -1))


def prolong(field):
    return jnp.repeat(jnp.repeat(jnp.repeat(field, 2, axis=-3), 2, axis=-2), 2, axis=-1)


def reference(source, cell_class, class_conductivity, layer_of_depth, inverses):
    sigma0 = jnp.zeros(cell_class.shape, class_conductivity.dtype)
    for index in range(NCLASS):
        sigma0 = sigma0 + jnp.where(cell_class == index, class_conductivity[index], 0.0)
    sigma1 = restrict(sigma0)
    layers0 = layer_of_depth
    layers1 = layer_of_depth[::2]
    rhs0 = source
    x0 = smooth(rhs0, inverses, layers0, 0)
    rhs1 = restrict(rhs0 - apply_operator(x0, sigma0, 0))
    x1 = smooth(rhs1, inverses, layers1, 1)
    x1 = x1 + smooth(rhs1 - apply_operator(x1, sigma1, 1), inverses, layers1, 1)
    x0 = x0 + prolong(x1)
    x0 = x0 + smooth(rhs0 - apply_operator(x0, sigma0, 0), inverses, layers0, 0)
    return x0
```

```python
import functools

import jax
import jax.numpy as jnp
from jax import lax
from jax.experimental import pallas as pl
from jax.experimental.pallas import tpu as pltpu
from jax.sharding import PartitionSpec as P

damping = 0.8
MESH = pl.DeviceIdType.MESH
f32 = jnp.float32
bf16 = jnp.bfloat16


def roll(x, shift, axis):
    shift = shift % x.shape[axis]
    return x if shift == 0 else pltpu.roll(x, shift, axis)


def iota(shape, axis):
    return lax.broadcasted_iota(jnp.int32, shape, axis)


def split(x):
    hi = x.astype(bf16)
    return hi, (x - hi.astype(f32)).astype(bf16)


def dot(a, b):
    return jnp.dot(a, b, preferred_element_type=f32)


def permute(x, matrix):
    hi, lo = split(x)
    return dot(hi, matrix) + dot(lo, matrix)


def pick_rows(x, places):
    row = iota(x.shape, 1)
    out = jnp.zeros_like(x)
    for shift in range(8):
        rows = [s for s in range(8) if places[s] is not None and (s - places[s]) % 8 == shift]
        if rows:
            mask = functools.reduce(jnp.logical_or, [row == s for s in rows])
            out = jnp.where(mask, roll(x, shift, 1), out)
    return out


def pair_rows(x):
    tiles = []
    for t in range(x.shape[1] // 16):
        low, high = x[:, 16 * t : 16 * t + 8], x[:, 16 * t + 8 : 16 * t + 16]
        low = low + roll(low, 7, 1)
        high = high + roll(high, 7, 1)
        tiles.append(pick_rows(low, [0, 2, 4, 6] + [None] * 4) + pick_rows(high, [None] * 4 + [0, 2, 4, 6]))
    return jnp.concatenate(tiles, axis=1)


def repeat_rows(x):
    tiles = []
    for t in range(x.shape[1] // 8):
        tile = x[:, 8 * t : 8 * t + 8]
        tiles.append(pick_rows(tile, [0, 0, 1, 1, 2, 2, 3, 3]))
        tiles.append(pick_rows(tile, [4, 4, 5, 5, 6, 6, 7, 7]))
    return jnp.concatenate(tiles, axis=1)


def first_half(shape, half):
    lane = iota(shape, len(shape) - 1)
    mask = lane < half
    for start in range(2 * half, shape[-1], 2 * half):
        mask = mask | ((lane >= start) & (lane < start + half))
    return mask


def swap_tiles(v0, v1):
    low = iota(v0.shape, 1) < 4
    return jnp.where(low, v0, roll(v1, 4, 1)), jnp.where(low, roll(v0, 4, 1), v1)


def swap_lanes(a, b, half):
    mask = first_half(a.shape, half)
    return jnp.where(mask, a, roll(b, half, 1)), jnp.where(mask, roll(a, -half, 1), b)


def smooth(field, out_ref, w_hi, w_lo, ids, half, scale):
    comps, sx, sy, nz = field.shape
    rows = comps * 16
    pairs = [(xb, p) for xb in range(sx // 4) for p in range(sy // 8)]
    columns = []
    for xb, p in pairs:
        v = field[:, 4 * xb : 4 * xb + 4, 8 * p : 8 * p + 8, :].reshape(comps * 2, 2, 8, nz)
        u0, u1 = swap_tiles(v[:, 0], v[:, 1])
        even, odd = swap_lanes(u0.reshape(rows, nz), u1.reshape(rows, nz), half)
        columns.append(jnp.concatenate([even, odd], axis=0))
    x = jnp.concatenate(columns, axis=1)
    hi, lo = split(x)
    size = 2 * rows
    every = dot(w_hi[...], hi) + dot(w_lo[...], hi) + dot(w_hi[...], lo)
    ids = jnp.concatenate([ids] * len(pairs), axis=1)
    total = jnp.zeros_like(x)
    for layer in range(w_hi.shape[0] // size):
        total = jnp.where(ids == layer, every[layer * size : (layer + 1) * size], total)
    total = total * scale
    for at, (xb, p) in enumerate(pairs):
        block = total[:, at * nz : (at + 1) * nz]
        u0, u1 = swap_lanes(block[:rows], block[rows:], half)
        v0, v1 = swap_tiles(u0.reshape(comps * 2, 8, nz), u1.reshape(comps * 2, 8, nz))
        v = jnp.stack([v0, v1], axis=1).reshape(comps, 4, 8, nz)
        out_ref[:, 4 * xb : 4 * xb + 4, 8 * p : 8 * p + 8, :] = v


def beside_z_fine(u):
    nz = u.shape[-1]
    q = nz // 4
    lane = iota(u.shape, u.ndim - 1)
    ax = u.ndim - 1
    other = jnp.where(
        lane < 2 * q,
        jnp.where(lane < q, roll(u, q + 1, ax), roll(u, -q, ax)),
        jnp.where(lane < 3 * q, roll(u, q, ax), roll(u, -q - 1, ax)),
    )
    other = jnp.where((lane == 0) | (lane == nz - 1), 0.0, other)
    return roll(u, 2 * q, ax) + other


def beside_z_coarse(u):
    nz = u.shape[-1]
    q = nz // 4
    lane = iota(u.shape, u.ndim - 1)
    ax = u.ndim - 1
    mask = first_half(u.shape, q)
    total = jnp.where(mask, roll(u, -q, ax), roll(u, q, ax))
    other = jnp.where(mask, roll(u, 1 - q, ax), roll(u, q - 1, ax))
    edge = (lane == 0) | (lane == 2 * q - 1) | (lane == 2 * q) | (lane == nz - 1)
    return total + jnp.where(edge, 0.0, other)


def residual(b, u, sigma, beside_z, factor):
    comps, sx, sy, nz = u.shape
    half = comps // 2
    flat = u.reshape(comps * sx, sy, nz)
    row = iota(flat.shape, 1)
    near = jnp.where(row == 0, 0.0, roll(flat, 1, 1)) + jnp.where(row == sy - 1, 0.0, roll(flat, -1, 1))
    near = (near + beside_z(flat)).reshape(u.shape)
    zero = jnp.zeros((comps, 1, sy, nz), f32)
    near = near + jnp.concatenate([zero, u[:, :-1]], axis=1) + jnp.concatenate([u[:, 1:], zero], axis=1)
    out = b - (6.0 * u - near) * factor
    turned = jnp.concatenate([sigma[None] * u[half:], -(sigma[None] * u[:half])], axis=0)
    return out + turned


def add_faces(r, faces_x, faces_y, factor):
    comps, sx, sy, nz = r.shape
    row = iota((comps * sx, sy, nz), 1)
    flat = r.reshape(comps * sx, sy, nz)
    flat = flat + jnp.where(row == 0, faces_y[0] * factor, 0.0) + jnp.where(row == sy - 1, faces_y[1] * factor, 0.0)
    r = flat.reshape(r.shape)
    low = r[:, :1] + faces_x[0][:, None] * factor
    high = r[:, sx - 1 :] + faces_x[1][:, None] * factor
    return jnp.concatenate([low, r[:, 1 : sx - 1], high], axis=1)


def restrict(u):
    comps, sx, sy, nz = u.shape
    v = u.reshape(comps * sx // 2, 2, sy, nz)
    v = v[:, 0] + v[:, 1]
    v = pair_rows(v)
    v = (v + roll(v, nz // 2, 2)) * 0.125
    return v.reshape(comps, sx // 2, sy // 2, nz)


def kernel(
    axes, sizes, src, cls, cond, depth, inv, out,
    w_hi, w_lo, b0, x0, r0, sig0, sig1, b1, x1, r1, d1,
    send_x, recv_x, send_y, recv_y, csend_x, crecv_x, csend_y, crecv_y, send_sem, recv_sem,
):
    comps, sx, sy, nz = src.shape
    me = [lax.axis_index(a) for a in axes]
    has = [me[0] > 0, me[0] < sizes[0] - 1, me[1] > 0, me[1] < sizes[1] - 1]

    def device(d):
        n = sizes[d // 2]
        return {axes[d // 2]: lax.rem(me[d // 2] + (n - 1 if d % 2 == 0 else 1), n)}

    barrier = pltpu.get_barrier_semaphore()
    for d in range(4):
        @pl.when(has[d])
        def _(d=d):
            pl.semaphore_signal(barrier, inc=1, device_id=device(d), device_id_type=MESH)

        @pl.when(jnp.logical_not(has[d]))
        def _(d=d):
            for ref in [(recv_x, crecv_x), (recv_y, crecv_y)][d // 2]:
                if ref is recv_x or ref is recv_y:
                    ref[d % 2] = jnp.zeros(ref.shape[1:], f32)
                else:
                    for e in range(2):
                        ref[e, d % 2] = jnp.zeros(ref.shape[2:], f32)

    def copy(e, d):
        if d < 2:
            s, r = (send_x, recv_x) if e == 0 else (csend_x.at[e - 1], crecv_x.at[e - 1])
        else:
            s, r = (send_y, recv_y) if e == 0 else (csend_y.at[e - 1], crecv_y.at[e - 1])
        k = d % 2
        return pltpu.make_async_remote_copy(
            src_ref=s.at[k], dst_ref=r.at[1 - k], send_sem=send_sem.at[e, d], recv_sem=recv_sem.at[e, d ^ 1],
            device_id=device(d), device_id_type=MESH,
        )

    def start(e, u):
        c, ux, uy, _ = u.shape
        sxr, syr = (send_x, send_y) if e == 0 else (csend_x.at[e - 1], csend_y.at[e - 1])
        sxr[0] = u[:, 0]
        sxr[1] = u[:, ux - 1]
        flat = u.reshape(c * ux, uy, nz)
        syr[0] = flat[:, 0:1]
        syr[1] = flat[:, uy - 1 : uy]
        for d in range(4):
            @pl.when(has[d])
            def _(d=d):
                copy(e, d).start()

    def finish(e):
        for d in range(4):
            @pl.when(has[d])
            def _(d=d):
                copy(e, d ^ 1).wait_recv()
                copy(e, d).wait_send()

    q = nz // 4
    def z_of(lane):
        zi = jnp.where(lane >= 2 * q, 1, 0)
        rest = lane - 2 * q * zi
        zic = jnp.where(rest >= q, 1, 0)
        return 4 * (rest - q * zic) + 2 * zic + zi
    to_lanes = jnp.where(iota((nz, nz), 0) == z_of(iota((nz, nz), 1)), 1.0, 0.0).astype(bf16)
    from_lanes = jnp.where(iota((nz, nz), 1) == z_of(iota((nz, nz), 0)), 1.0, 0.0).astype(bf16)

    lane = iota((1, nz), 1)
    zb = z_of(lane - jnp.where(lane >= 2 * q, 2 * q, 0)) // 2
    ids0 = jnp.zeros((1, nz), jnp.int32)
    for k in range(depth.shape[0]):
        ids0 = jnp.where(zb == k, depth[k], ids0)
    ids1 = jnp.where(first_half((1, nz), q), ids0, roll(ids0, q, 1))

    layers, size, _ = inv.shape
    mid = size // 2
    def k_of(j):
        return jnp.where(j < mid, 2 * j, 2 * (j - mid) + 1)
    right = jnp.where(iota((size, size), 0) == k_of(iota((size, size), 1)), 1.0, 0.0).astype(bf16)
    left = jnp.where(iota((size, size), 1) == k_of(iota((size, size), 0)), 1.0, 0.0).astype(bf16)
    for part, ref in zip(split(inv[...].reshape(layers * size, size)), (w_hi, w_lo)):
        turned = dot(part, right).astype(bf16)
        for layer in range(layers):
            at = slice(layer * size, (layer + 1) * size)
            ref[at, :] = dot(left, turned[at]).astype(bf16)

    b0[...] = permute(src[...].reshape(-1, nz), to_lanes).reshape(src.shape)
    kinds = dot(cls[...].reshape(-1, nz).astype(f32).astype(bf16), to_lanes)
    sigma = jnp.zeros_like(kinds)
    for k in range(cond.shape[0]):
        sigma = jnp.where(kinds == float(k), cond[k], sigma)
    sigma = sigma.reshape(sx, sy, nz)
    sig0[...] = sigma
    sig1[...] = restrict(sigma[None])[0]

    smooth(b0[...], x0, w_hi, w_lo, ids0, nz // 2, damping)
    pl.semaphore_wait(barrier, sum(jnp.where(h, 1, 0) for h in has))
    start(0, x0[...])
    r0[...] = residual(b0[...], x0[...], sig0[...], beside_z_fine, 1.0)
    finish(0)
    b1[...] = restrict(add_faces(r0[...], recv_x, recv_y, 1.0))

    smooth(b1[...], x1, w_hi, w_lo, ids1, q, damping * 4.0)
    start(1, x1[...])
    r1[...] = residual(b1[...], x1[...], sig1[...], beside_z_coarse, 0.25)
    finish(1)
    smooth(add_faces(r1[...], crecv_x.at[0], crecv_y.at[0], 0.25), d1, w_hi, w_lo, ids1, q, damping * 4.0)
    xc = x1[...] + d1[...]
    start(2, xc)
    cx, cy = sx // 2, sy // 2
    spread = repeat_rows(xc.reshape(comps * cx, cy, nz)).reshape(comps, cx, 1, sy, nz)
    spread = jnp.concatenate([spread, spread], axis=2).reshape(src.shape)
    x0[...] = x0[...] + spread
    r0[...] = residual(b0[...], x0[...], sig0[...], beside_z_fine, 1.0)
    finish(2)
    faces_x = [recv_x[k] + repeat_rows(crecv_x[1, k]) for k in range(2)]
    faces_y = []
    for k in range(2):
        face = crecv_y[1, k].reshape(comps * cx, 1, 1, nz)
        face = jnp.concatenate([face, face], axis=1).reshape(comps * sx, 1, nz)
        faces_y.append(recv_y[k] + face)
    smooth(add_faces(r0[...], faces_x, faces_y, 1.0), r0, w_hi, w_lo, ids0, nz // 2, damping)
    out[...] = permute((x0[...] + r0[...]).reshape(-1, nz), from_lanes).reshape(out.shape)


def solution(mesh):
    axes = ("gx", "gy")
    sizes = tuple(mesh.shape[a] for a in axes)

    def per_device(source, cell_class, class_conductivity, layer_of_depth, inverses):
        comps, sx, sy, nz = source.shape
        layers, size, _ = inverses.shape
        cx, cy = sx // 2, sy // 2
        vmem = pl.BlockSpec(memory_space=pltpu.VMEM)
        smem = pl.BlockSpec(memory_space=pltpu.SMEM)
        fine, coarse = (comps, sx, sy, nz), (comps, cx, cy, nz)
        scratch = [
            ((layers * size, size), bf16), ((layers * size, size), bf16),
            (fine, f32), (fine, f32), (fine, f32), ((sx, sy, nz), f32), ((cx, cy, nz), f32),
            (coarse, f32), (coarse, f32), (coarse, f32), (coarse, f32),
        ]
        scratch += [((2, comps, sy, nz), f32)] * 2 + [((2, comps * sx, 1, nz), f32)] * 2
        scratch += [((2, 2, comps, cy, nz), f32)] * 2 + [((2, 2, comps * cx, 1, nz), f32)] * 2
        return pl.pallas_call(
            functools.partial(kernel, axes, sizes),
            out_shape=jax.ShapeDtypeStruct(source.shape, f32),
            in_specs=[vmem, vmem, smem, smem, vmem],
            out_specs=vmem,
            scratch_shapes=[pltpu.VMEM(s, t) for s, t in scratch]
            + [pltpu.SemaphoreType.DMA((3, 4)), pltpu.SemaphoreType.DMA((3, 4))],
            compiler_params=pltpu.CompilerParams(
                collective_id=0, has_side_effects=True, vmem_limit_bytes=50 * 2**20
            ),
        )(source, cell_class, class_conductivity, layer_of_depth, inverses)

    return jax.shard_map(
        per_device,
        mesh=mesh,
        in_specs=(P(None, "gx", "gy", None), P("gx", "gy", None), P(), P(), P()),
        out_specs=P(None, "gx", "gy", None),
        check_vma=False,
    )
```

```python
import functools

import jax
import jax.numpy as jnp
from jax import lax
from jax.experimental import pallas as pl
from jax.experimental.pallas import tpu as pltpu
from jax.sharding import PartitionSpec as P

damping = 0.8
MESH = pl.DeviceIdType.MESH
f32 = jnp.float32
bf16 = jnp.bfloat16


def roll(x, shift, axis):
    shift = shift % x.shape[axis]
    return x if shift == 0 else pltpu.roll(x, shift, axis)


def iota(shape, axis):
    return lax.broadcasted_iota(jnp.int32, shape, axis)


def split(x):
    hi = x.astype(bf16)
    return hi, (x - hi.astype(f32)).astype(bf16)


def dot(a, b):
    return jnp.dot(a, b, preferred_element_type=f32)


def permute(x, matrix):
    hi, lo = split(x)
    return dot(hi, matrix) + dot(lo, matrix)


def pick_rows(x, places):
    row = iota(x.shape, 1)
    out = jnp.zeros_like(x)
    for shift in range(8):
        rows = [s for s in range(8) if places[s] is not None and (s - places[s]) % 8 == shift]
        if rows:
            mask = functools.reduce(jnp.logical_or, [row == s for s in rows])
            out = jnp.where(mask, roll(x, shift, 1), out)
    return out


def pair_rows(x):
    tiles = []
    for t in range(x.shape[1] // 16):
        low, high = x[:, 16 * t : 16 * t + 8], x[:, 16 * t + 8 : 16 * t + 16]
        low = low + roll(low, 7, 1)
        high = high + roll(high, 7, 1)
        tiles.append(pick_rows(low, [0, 2, 4, 6] + [None] * 4) + pick_rows(high, [None] * 4 + [0, 2, 4, 6]))
    return jnp.concatenate(tiles, axis=1)


def repeat_rows(x):
    tiles = []
    for t in range(x.shape[1] // 8):
        tile = x[:, 8 * t : 8 * t + 8]
        tiles.append(pick_rows(tile, [0, 0, 1, 1, 2, 2, 3, 3]))
        tiles.append(pick_rows(tile, [4, 4, 5, 5, 6, 6, 7, 7]))
    return jnp.concatenate(tiles, axis=1)


def first_half(shape, half):
    lane = iota(shape, len(shape) - 1)
    mask = lane < half
    for start in range(2 * half, shape[-1], 2 * half):
        mask = mask | ((lane >= start) & (lane < start + half))
    return mask


def swap_tiles(v0, v1):
    low = iota(v0.shape, 1) < 4
    return jnp.where(low, v0, roll(v1, 4, 1)), jnp.where(low, roll(v0, 4, 1), v1)


def swap_lanes(a, b, half):
    mask = first_half(a.shape, half)
    return jnp.where(mask, a, roll(b, half, 1)), jnp.where(mask, roll(a, -half, 1), b)


def masked(x, ids, layers):
    tiles = x.reshape(-1, 16, x.shape[1])
    out = []
    for layer in range(layers):
        mask = jnp.broadcast_to(jnp.where(ids == layer, 1.0, 0.0), (16, x.shape[1])).astype(bf16)
        out.append((tiles * mask[None]).reshape(x.shape))
    return jnp.concatenate(out, axis=0)


def smooth(field, out_ref, w, ids, half, scale, block_in, block_out):
    comps, sx, sy, nz = field.shape
    rows = comps * 16
    size = 2 * rows
    layers = w.shape[1] // size
    pairs = [(xb, p) for xb in range(sx // 4) for p in range(sy // 8)]
    for at, (xb, p) in enumerate(pairs):
        v = field[:, 4 * xb : 4 * xb + 4, 8 * p : 8 * p + 8, :].reshape(comps * 2, 2, 8, nz)
        u0, u1 = swap_tiles(v[:, 0], v[:, 1])
        even, odd = swap_lanes(u0.reshape(rows, nz), u1.reshape(rows, nz), half)
        block_in[at, pl.ds(0, rows, stride=2), :] = even
        block_in[at, pl.ds(1, rows, stride=2), :] = odd
    n = len(pairs) * nz
    hi, lo = split(jnp.concatenate([block_in[at] for at in range(len(pairs))], axis=1))
    ids = jnp.concatenate([ids] * len(pairs), axis=1)
    if n < 256:
        x = masked(jnp.concatenate([hi, lo], axis=1), jnp.concatenate([ids, ids], axis=1), layers)
        total = dot(w[...], x)
        total = total[:size] + total[size:]
        total = total[:, :n] + total[:, n:]
    else:
        total = dot(w[...], masked(hi, ids, layers))
        total = total[:size] + total[size:] + dot(w[:size, :], masked(lo, ids, layers))
    total = total * scale
    for at, (xb, p) in enumerate(pairs):
        block_out[at] = total[:, at * nz : (at + 1) * nz]
        even = block_out[at, pl.ds(0, rows, stride=2), :]
        odd = block_out[at, pl.ds(1, rows, stride=2), :]
        u0, u1 = swap_lanes(even, odd, half)
        v0, v1 = swap_tiles(u0.reshape(comps * 2, 8, nz), u1.reshape(comps * 2, 8, nz))
        v = jnp.stack([v0, v1], axis=1).reshape(comps, 4, 8, nz)
        out_ref[:, 4 * xb : 4 * xb + 4, 8 * p : 8 * p + 8, :] = v


def beside_z_fine(u):
    nz = u.shape[-1]
    q = nz // 4
    lane = iota(u.shape, u.ndim - 1)
    ax = u.ndim - 1
    other = jnp.where(
        lane < 2 * q,
        jnp.where(lane < q, roll(u, q + 1, ax), roll(u, -q, ax)),
        jnp.where(lane < 3 * q, roll(u, q, ax), roll(u, -q - 1, ax)),
    )
    other = jnp.where((lane == 0) | (lane == nz - 1), 0.0, other)
    return roll(u, 2 * q, ax) + other


def beside_z_coarse(u):
    nz = u.shape[-1]
    q = nz // 4
    lane = iota(u.shape, u.ndim - 1)
    ax = u.ndim - 1
    mask = first_half(u.shape, q)
    total = jnp.where(mask, roll(u, -q, ax), roll(u, q, ax))
    other = jnp.where(mask, roll(u, 1 - q, ax), roll(u, q - 1, ax))
    edge = (lane == 0) | (lane == 2 * q - 1) | (lane == 2 * q) | (lane == nz - 1)
    return total + jnp.where(edge, 0.0, other)


def residual(b, u, sigma, beside_z, factor):
    comps, sx, sy, nz = u.shape
    half = comps // 2
    flat = u.reshape(comps * sx, sy, nz)
    row = iota(flat.shape, 1)
    near = jnp.where(row == 0, 0.0, roll(flat, 1, 1)) + jnp.where(row == sy - 1, 0.0, roll(flat, -1, 1))
    near = (near + beside_z(flat)).reshape(u.shape)
    zero = jnp.zeros((comps, 1, sy, nz), f32)
    near = near + jnp.concatenate([zero, u[:, :-1]], axis=1) + jnp.concatenate([u[:, 1:], zero], axis=1)
    out = b - (6.0 * u - near) * factor
    turned = jnp.concatenate([sigma[None] * u[half:], -(sigma[None] * u[:half])], axis=0)
    return out + turned


def add_faces(r, faces_x, faces_y, factor):
    comps, sx, sy, nz = r.shape
    row = iota((comps * sx, sy, nz), 1)
    flat = r.reshape(comps * sx, sy, nz)
    flat = flat + jnp.where(row == 0, faces_y[0] * factor, 0.0) + jnp.where(row == sy - 1, faces_y[1] * factor, 0.0)
    r = flat.reshape(r.shape)
    low = r[:, :1] + faces_x[0][:, None] * factor
    high = r[:, sx - 1 :] + faces_x[1][:, None] * factor
    return jnp.concatenate([low, r[:, 1 : sx - 1], high], axis=1)


def restrict(u):
    comps, sx, sy, nz = u.shape
    v = u.reshape(comps * sx // 2, 2, sy, nz)
    v = v[:, 0] + v[:, 1]
    v = pair_rows(v)
    v = (v + roll(v, nz // 2, 2)) * 0.125
    return v.reshape(comps, sx // 2, sy // 2, nz)


def kernel(
    axes, sizes, src_hbm, cls_hbm, cond_hbm, depth_hbm, inv_hbm, out,
    src, cls, cond, depth, inv, in_sem, block_in, block_out, w, b0, x0, r0, sig0, sig1, b1, x1, r1, d1,
    send_x, recv_x, send_y, recv_y, csend_x, crecv_x, csend_y, crecv_y, send_sem, recv_sem,
):
    comps, sx, sy, nz = src.shape
    named = ((src_hbm, src), (cls_hbm, cls), (cond_hbm, cond), (depth_hbm, depth), (inv_hbm, inv))
    loads = [pltpu.make_async_copy(a, b, in_sem.at[i]) for i, (a, b) in enumerate(named)]
    for load in loads:
        load.start()
    me = [lax.axis_index(a) for a in axes]
    has = [me[0] > 0, me[0] < sizes[0] - 1, me[1] > 0, me[1] < sizes[1] - 1]

    def device(d):
        n = sizes[d // 2]
        return {axes[d // 2]: lax.rem(me[d // 2] + (n - 1 if d % 2 == 0 else 1), n)}

    barrier = pltpu.get_barrier_semaphore()
    for d in range(4):
        @pl.when(has[d])
        def _(d=d):
            pl.semaphore_signal(barrier, inc=1, device_id=device(d), device_id_type=MESH)

        @pl.when(jnp.logical_not(has[d]))
        def _(d=d):
            for ref in [(recv_x, crecv_x), (recv_y, crecv_y)][d // 2]:
                if ref is recv_x or ref is recv_y:
                    ref[d % 2] = jnp.zeros(ref.shape[1:], f32)
                else:
                    for e in range(2):
                        ref[e, d % 2] = jnp.zeros(ref.shape[2:], f32)

    def copy(e, d):
        if d < 2:
            s, r = (send_x, recv_x) if e == 0 else (csend_x.at[e - 1], crecv_x.at[e - 1])
        else:
            s, r = (send_y, recv_y) if e == 0 else (csend_y.at[e - 1], crecv_y.at[e - 1])
        k = d % 2
        return pltpu.make_async_remote_copy(
            src_ref=s.at[k], dst_ref=r.at[1 - k], send_sem=send_sem.at[e, d], recv_sem=recv_sem.at[e, d ^ 1],
            device_id=device(d), device_id_type=MESH,
        )

    def start(e, u):
        c, ux, uy, _ = u.shape
        sxr, syr = (send_x, send_y) if e == 0 else (csend_x.at[e - 1], csend_y.at[e - 1])
        sxr[0] = u[:, 0]
        sxr[1] = u[:, ux - 1]
        flat = u.reshape(c * ux, uy, nz)
        syr[0] = flat[:, 0:1]
        syr[1] = flat[:, uy - 1 : uy]
        for d in range(4):
            @pl.when(has[d])
            def _(d=d):
                copy(e, d).start()

    def finish(e):
        for d in range(4):
            @pl.when(has[d])
            def _(d=d):
                copy(e, d ^ 1).wait_recv()
                copy(e, d).wait_send()

    q = nz // 4
    def z_of(lane):
        zi = jnp.where(lane >= 2 * q, 1, 0)
        rest = lane - 2 * q * zi
        zic = jnp.where(rest >= q, 1, 0)
        return 4 * (rest - q * zic) + 2 * zic + zi
    to_lanes = jnp.where(iota((nz, nz), 0) == z_of(iota((nz, nz), 1)), 1.0, 0.0).astype(bf16)
    from_lanes = jnp.where(iota((nz, nz), 1) == z_of(iota((nz, nz), 0)), 1.0, 0.0).astype(bf16)

    loads[0].wait()
    b0[...] = permute(src[...].reshape(-1, nz), to_lanes).reshape(src.shape)
    loads[1].wait()
    kinds = dot(cls[...].reshape(-1, nz).astype(f32).astype(bf16), to_lanes)
    loads[2].wait()
    sigma = jnp.zeros_like(kinds)
    for k in range(cond.shape[0]):
        sigma = jnp.where(kinds == float(k), cond[k], sigma)
    sigma = sigma.reshape(sx, sy, nz)
    sig0[...] = sigma
    sig1[...] = restrict(sigma[None])[0]

    loads[3].wait()
    lane = iota((1, nz), 1)
    zb = z_of(lane - jnp.where(lane >= 2 * q, 2 * q, 0)) // 2
    ids0 = jnp.zeros((1, nz), jnp.int32)
    for k in range(depth.shape[0]):
        ids0 = jnp.where(zb == k, depth[k], ids0)
    ids1 = jnp.where(first_half((1, nz), q), ids0, roll(ids0, q, 1))

    loads[4].wait()
    layers, size, _ = inv.shape
    hi, lo = split(jnp.concatenate([inv[layer] for layer in range(layers)], axis=1))
    w[:size, :] = hi
    w[size:, :] = lo

    smooth(b0[...], x0, w, ids0, nz // 2, damping, block_in, block_out)
    pl.semaphore_wait(barrier, sum(jnp.where(h, 1, 0) for h in has))
    start(0, x0[...])
    r0[...] = residual(b0[...], x0[...], sig0[...], beside_z_fine, 1.0)
    finish(0)
    b1[...] = restrict(add_faces(r0[...], recv_x, recv_y, 1.0))

    smooth(b1[...], x1, w, ids1, q, damping * 4.0, block_in, block_out)
    start(1, x1[...])
    r1[...] = residual(b1[...], x1[...], sig1[...], beside_z_coarse, 0.25)
    finish(1)
    smooth(add_faces(r1[...], crecv_x.at[0], crecv_y.at[0], 0.25), d1, w, ids1, q, damping * 4.0, block_in, block_out)
    xc = x1[...] + d1[...]
    start(2, xc)
    cx, cy = sx // 2, sy // 2
    spread = repeat_rows(xc.reshape(comps * cx, cy, nz)).reshape(comps, cx, 1, sy, nz)
    spread = jnp.concatenate([spread, spread], axis=2).reshape(src.shape)
    x0[...] = x0[...] + spread
    r0[...] = residual(b0[...], x0[...], sig0[...], beside_z_fine, 1.0)
    finish(2)
    faces_x = [recv_x[k] + repeat_rows(crecv_x[1, k]) for k in range(2)]
    faces_y = []
    for k in range(2):
        face = crecv_y[1, k].reshape(comps * cx, 1, 1, nz)
        face = jnp.concatenate([face, face], axis=1).reshape(comps * sx, 1, nz)
        faces_y.append(recv_y[k] + face)
    smooth(add_faces(r0[...], faces_x, faces_y, 1.0), r0, w, ids0, nz // 2, damping, block_in, block_out)
    out[...] = permute((x0[...] + r0[...]).reshape(-1, nz), from_lanes).reshape(out.shape)


def solution(mesh):
    axes = ("gx", "gy")
    sizes = tuple(mesh.shape[a] for a in axes)

    def per_device(source, cell_class, class_conductivity, layer_of_depth, inverses):
        comps, sx, sy, nz = source.shape
        layers, size, _ = inverses.shape
        cx, cy = sx // 2, sy // 2
        vmem = pl.BlockSpec(memory_space=pltpu.VMEM)
        hbm = pl.BlockSpec(memory_space=pltpu.HBM)
        fine, coarse = (comps, sx, sy, nz), (comps, cx, cy, nz)
        scratch = [
            ((sx // 4 * (sy // 8), size, nz), f32), ((sx // 4 * (sy // 8), size, nz), f32),
            ((2 * size, layers * size), bf16), (fine, f32), (fine, f32), (fine, f32), ((sx, sy, nz), f32), ((cx, cy, nz), f32),
            (coarse, f32), (coarse, f32), (coarse, f32), (coarse, f32),
        ]
        scratch += [((2, comps, sy, nz), f32)] * 2 + [((2, comps * sx, 1, nz), f32)] * 2
        scratch += [((2, 2, comps, cy, nz), f32)] * 2 + [((2, 2, comps * cx, 1, nz), f32)] * 2
        return pl.pallas_call(
            functools.partial(kernel, axes, sizes),
            out_shape=jax.ShapeDtypeStruct(source.shape, f32),
            in_specs=[hbm] * 5,
            out_specs=vmem,
            scratch_shapes=[pltpu.VMEM(source.shape, f32), pltpu.VMEM(cell_class.shape, jnp.int32)]
            + [pltpu.SMEM(class_conductivity.shape, f32), pltpu.SMEM(layer_of_depth.shape, jnp.int32)]
            + [pltpu.VMEM(inverses.shape, f32), pltpu.SemaphoreType.DMA((5,))]
            + [pltpu.VMEM(s, t) for s, t in scratch]
            + [pltpu.SemaphoreType.DMA((3, 4)), pltpu.SemaphoreType.DMA((3, 4))],
            compiler_params=pltpu.CompilerParams(
                collective_id=0, has_side_effects=True, vmem_limit_bytes=50 * 2**20
            ),
        )(source, cell_class, class_conductivity, layer_of_depth, inverses)

    return jax.shard_map(
        per_device,
        mesh=mesh,
        in_specs=(P(None, "gx", "gy", None), P("gx", "gy", None), P(), P(), P()),
        out_specs=P(None, "gx", "gy", None),
        check_vma=False,
    )
```

```python
import functools

import jax
import jax.numpy as jnp
from jax import lax
from jax.experimental import pallas as pl
from jax.experimental.pallas import tpu as pltpu
from jax.sharding import PartitionSpec as P

damping = 0.8
MESH = pl.DeviceIdType.MESH
f32 = jnp.float32
bf16 = jnp.bfloat16


def roll(x, shift, axis):
    shift = shift % x.shape[axis]
    return x if shift == 0 else pltpu.roll(x, shift, axis)


def iota(shape, axis):
    return lax.broadcasted_iota(jnp.int32, shape, axis)


def split(x):
    hi = x.astype(bf16)
    return hi, (x - hi.astype(f32)).astype(bf16)


def dot(a, b):
    return jnp.dot(a, b, preferred_element_type=f32)


def permute(x, matrix):
    hi, lo = split(x)
    return dot(hi, matrix) + dot(lo, matrix)


def pair_rows(x, t):
    n = x.shape[0]
    t[:n, :] = x
    return t[pl.ds(0, n // 2, stride=2), :] + t[pl.ds(1, n // 2, stride=2), :]


def repeat_rows(x, t):
    n = x.shape[0]
    t[pl.ds(0, n, stride=2), :] = x
    t[pl.ds(1, n, stride=2), :] = x
    return t[: 2 * n, :]


def pack(x):
    n = x.shape[0] // 2
    return jnp.where(iota((n,) + x.shape[1:], x.ndim - 1) < x.shape[-1] // 2, x[:n], x[n:])


def unpack(x):
    half = x.shape[-1] // 2
    turned = roll(x, half, x.ndim - 1)
    first = iota(x.shape, x.ndim - 1) < half
    return jnp.concatenate([jnp.where(first, x, turned), jnp.where(first, turned, x)], axis=0)


def first_half(shape, half):
    lane = iota(shape, len(shape) - 1)
    mask = lane < half
    for start in range(2 * half, shape[-1], 2 * half):
        mask = mask | ((lane >= start) & (lane < start + half))
    return mask


def swap_tiles(v0, v1):
    low = iota(v0.shape, 1) < 4
    return jnp.where(low, v0, roll(v1, 4, 1)), jnp.where(low, roll(v0, 4, 1), v1)


def swap_lanes(a, b, half):
    mask = first_half(a.shape, half)
    return jnp.where(mask, a, roll(b, half, 1)), jnp.where(mask, roll(a, -half, 1), b)


def masked(x, ids, layers):
    tiles = x.reshape(-1, 16, x.shape[1])
    out = []
    for layer in range(layers):
        mask = jnp.broadcast_to(jnp.where(ids == layer, 1.0, 0.0), (16, x.shape[1])).astype(bf16)
        out.append((tiles * mask[None]).reshape(x.shape))
    return jnp.concatenate(out, axis=0)


def smooth(field, out_ref, w, ids, half, scale, block_in, block_out):
    comps, sx, sy, nz = field.shape
    rows = comps * 16
    size = 2 * rows
    layers = w.shape[1] // size
    pairs = [(xb, p) for xb in range(sx // 4) for p in range(sy // 8)]
    for at, (xb, p) in enumerate(pairs):
        v = field[:, 4 * xb : 4 * xb + 4, 8 * p : 8 * p + 8, :].reshape(comps * 2, 2, 8, nz)
        u0, u1 = swap_tiles(v[:, 0], v[:, 1])
        even, odd = swap_lanes(u0.reshape(rows, nz), u1.reshape(rows, nz), half)
        block_in[at, pl.ds(0, rows, stride=2), :] = even
        block_in[at, pl.ds(1, rows, stride=2), :] = odd
    n = len(pairs) * nz
    hi, lo = split(jnp.concatenate([block_in[at] for at in range(len(pairs))], axis=1))
    ids = jnp.concatenate([ids] * len(pairs), axis=1)
    if n < 256:
        x = masked(jnp.concatenate([hi, lo], axis=1), jnp.concatenate([ids, ids], axis=1), layers)
        total = dot(w[...], x)
        total = total[:size] + total[size:]
        total = total[:, :n] + total[:, n:]
    else:
        total = dot(w[...], masked(hi, ids, layers))
        total = total[:size] + total[size:] + dot(w[:size, :], masked(lo, ids, layers))
    total = total * scale
    for at, (xb, p) in enumerate(pairs):
        block_out[at] = total[:, at * nz : (at + 1) * nz]
        even = block_out[at, pl.ds(0, rows, stride=2), :]
        odd = block_out[at, pl.ds(1, rows, stride=2), :]
        u0, u1 = swap_lanes(even, odd, half)
        v0, v1 = swap_tiles(u0.reshape(comps * 2, 8, nz), u1.reshape(comps * 2, 8, nz))
        v = jnp.stack([v0, v1], axis=1).reshape(comps, 4, 8, nz)
        out_ref[:, 4 * xb : 4 * xb + 4, 8 * p : 8 * p + 8, :] = v


def residual(b, u, sigma, beside_z, factor):
    comps, sx, sy, nz = u.shape
    half = comps // 2
    flat = u.reshape(comps * sx, sy, nz)
    row = iota(flat.shape, 1)
    near = jnp.where(row == 0, 0.0, roll(flat, 1, 1)) + jnp.where(row == sy - 1, 0.0, roll(flat, -1, 1))
    near = near.reshape(u.shape) + permute(flat.reshape(-1, nz), beside_z).reshape(u.shape)
    zero = jnp.zeros((comps, 1, sy, nz), f32)
    near = near + jnp.concatenate([zero, u[:, :-1]], axis=1) + jnp.concatenate([u[:, 1:], zero], axis=1)
    out = b - (6.0 * u - near) * factor
    turned = jnp.concatenate([sigma[None] * u[half:], -(sigma[None] * u[:half])], axis=0)
    return out + turned


def add_faces(r, faces_x, faces_y, factor):
    comps, sx, sy, nz = r.shape
    row = iota((comps * sx, sy, nz), 1)
    flat = r.reshape(comps * sx, sy, nz)
    flat = flat + jnp.where(row == 0, faces_y[0] * factor, 0.0) + jnp.where(row == sy - 1, faces_y[1] * factor, 0.0)
    r = flat.reshape(r.shape)
    low = r[:, :1] + faces_x[0][:, None] * factor
    high = r[:, sx - 1 :] + faces_x[1][:, None] * factor
    return jnp.concatenate([low, r[:, 1 : sx - 1], high], axis=1)


def restrict(u, t):
    comps, sx, sy, nz = u.shape
    v = u.reshape(comps * sx // 2, 2, sy, nz)
    v = pair_rows((v[:, 0] + v[:, 1]).reshape(-1, nz), t)
    v = (v + roll(v, nz // 2, 1)) * 0.125
    return v.reshape(comps, sx // 2, sy // 2, nz)


def kernel(
    axes, sizes, src_hbm, cls_hbm, cond_hbm, depth_hbm, inv_hbm, out,
    src, cls, cond, depth, inv, in_sem, block_in, block_out, w, b0, x0, r0, sig0, sig1, b1, x1, r1, d1, t,
    send_x, recv_x, send_y, recv_y, csend_x, crecv_x, csend_y, crecv_y, send_sem, recv_sem,
):
    comps, sx, sy, nz = src.shape
    named = ((src_hbm, src), (cls_hbm, cls), (cond_hbm, cond), (depth_hbm, depth), (inv_hbm, inv))
    loads = [pltpu.make_async_copy(a, b, in_sem.at[i]) for i, (a, b) in enumerate(named)]
    for load in loads:
        load.start()
    me = [lax.axis_index(a) for a in axes]
    has = [me[0] > 0, me[0] < sizes[0] - 1, me[1] > 0, me[1] < sizes[1] - 1]

    def device(d):
        n = sizes[d // 2]
        return {axes[d // 2]: lax.rem(me[d // 2] + (n - 1 if d % 2 == 0 else 1), n)}

    barrier = pltpu.get_barrier_semaphore()
    for d in range(4):
        @pl.when(has[d])
        def _(d=d):
            pl.semaphore_signal(barrier, inc=1, device_id=device(d), device_id_type=MESH)

        @pl.when(jnp.logical_not(has[d]))
        def _(d=d):
            for ref in [(recv_x, crecv_x), (recv_y, crecv_y)][d // 2]:
                if ref is recv_x or ref is recv_y:
                    ref[d % 2] = jnp.zeros(ref.shape[1:], f32)
                else:
                    for e in range(3):
                        ref[e, d % 2] = jnp.zeros(ref.shape[2:], f32)

    def copy(e, d):
        if d < 2:
            s, r = (send_x, recv_x) if e == 3 else (csend_x.at[e], crecv_x.at[e])
        else:
            s, r = (send_y, recv_y) if e == 3 else (csend_y.at[e], crecv_y.at[e])
        k = d % 2
        return pltpu.make_async_remote_copy(
            src_ref=s.at[k], dst_ref=r.at[1 - k], send_sem=send_sem.at[e, d], recv_sem=recv_sem.at[e, d ^ 1],
            device_id=device(d), device_id_type=MESH,
        )

    def launch(e):
        for d in range(4):
            @pl.when(has[d])
            def _(d=d):
                copy(e, d).start()

    def start(e, u):
        c, ux, uy, _ = u.shape
        flat = u.reshape(c * ux, uy, nz)
        for k in range(2):
            csend_x[e, k] = pack(u[:, k * (ux - 1)])
            csend_y[e, k] = pack(flat[:, k * (uy - 1) : k * (uy - 1) + 1])
        launch(e)

    def faces(e):
        return [unpack(crecv_x[e, k]) for k in range(2)], [unpack(crecv_y[e, k]) for k in range(2)]

    def finish(e):
        for d in range(4):
            @pl.when(has[d])
            def _(d=d):
                copy(e, d ^ 1).wait_recv()
                copy(e, d).wait_send()

    q = nz // 4
    def z_of(lane):
        zi = jnp.where(lane >= 2 * q, 1, 0)
        rest = lane - 2 * q * zi
        zic = jnp.where(rest >= q, 1, 0)
        return 4 * (rest - q * zic) + 2 * zic + zi
    to_lanes = jnp.where(iota((nz, nz), 0) == z_of(iota((nz, nz), 1)), 1.0, 0.0).astype(bf16)
    from_lanes = jnp.where(iota((nz, nz), 1) == z_of(iota((nz, nz), 0)), 1.0, 0.0).astype(bf16)

    beside0 = jnp.where(jnp.abs(z_of(iota((nz, nz), 0)) - z_of(iota((nz, nz), 1))) == 1, 1.0, 0.0).astype(bf16)
    def zc_of(lane):
        return z_of(lane - jnp.where(lane >= 2 * q, 2 * q, 0)) // 2
    near1 = jnp.abs(zc_of(iota((nz, nz), 0)) - zc_of(iota((nz, nz), 1))) == 1
    beside1 = jnp.where(near1 & (iota((nz, nz), 0) < 2 * q), 1.0, 0.0).astype(bf16)

    loads[0].wait()
    b0[...] = permute(src[...].reshape(-1, nz), to_lanes).reshape(src.shape)
    loads[1].wait()
    kinds = dot(cls[...].reshape(-1, nz).astype(f32).astype(bf16), to_lanes)
    loads[2].wait()
    sigma = jnp.zeros_like(kinds)
    for k in range(cond.shape[0]):
        sigma = jnp.where(kinds == float(k), cond[k], sigma)
    sigma = sigma.reshape(sx, sy, nz)
    sig0[...] = sigma
    sig1[...] = restrict(sigma[None], t)[0]

    loads[3].wait()
    lane = iota((1, nz), 1)
    zb = zc_of(lane)
    ids0 = jnp.zeros((1, nz), jnp.int32)
    for k in range(depth.shape[0]):
        ids0 = jnp.where(zb == k, depth[k], ids0)
    ids1 = jnp.where(first_half((1, nz), q), ids0, roll(ids0, q, 1))

    loads[4].wait()
    layers, size, _ = inv.shape
    hi, lo = split(jnp.concatenate([inv[layer] for layer in range(layers)], axis=1))
    w[:size, :] = hi
    w[size:, :] = lo

    smooth(b0[...], x0, w, ids0, nz // 2, damping, block_in, block_out)
    pl.semaphore_wait(barrier, sum(jnp.where(h, 1, 0) for h in has))
    flat = x0[...].reshape(comps * sx, sy, nz)
    for k in range(2):
        face = x0[:, k * (sx - 1)]
        face = pair_rows(face.reshape(comps * sy, nz), t).reshape(comps, sy // 2, nz)
        csend_x[0, k] = pack((face + roll(face, nz // 2, 2)) * 0.125)
        send_y[k] = flat[:, k * (sy - 1) : k * (sy - 1) + 1]
        face = send_y[k].reshape(comps * sx // 2, 2, 1, nz)
        face = face[:, 0] + face[:, 1]
        csend_y[0, k] = pack((face + roll(face, nz // 2, 2)) * 0.125)
        send_x[k] = x0[:, k * (sx - 1)]
    launch(0)
    r0[...] = residual(b0[...], x0[...], sig0[...], beside0, 1.0)
    b1[...] = restrict(r0[...], t)
    finish(0)
    launch(3)
    b1[...] = add_faces(b1[...], *faces(0), 1.0)

    smooth(b1[...], x1, w, ids1, q, damping * 4.0, block_in, block_out)
    start(1, x1[...])
    r1[...] = residual(b1[...], x1[...], sig1[...], beside1, 0.25)
    finish(1)
    smooth(add_faces(r1[...], *faces(1), 0.25), d1, w, ids1, q, damping * 4.0, block_in, block_out)
    xc = x1[...] + d1[...]
    start(2, xc)
    cx, cy = sx // 2, sy // 2
    spread = repeat_rows(xc.reshape(-1, nz), t).reshape(comps, cx, 1, sy, nz)
    spread = jnp.concatenate([spread, spread], axis=2).reshape(src.shape)
    x0[...] = x0[...] + spread
    r0[...] = residual(b0[...], x0[...], sig0[...], beside0, 1.0)
    finish(3)
    finish(2)
    faces_x, faces_y = faces(2)
    for k in range(2):
        faces_x[k] = recv_x[k] + repeat_rows(faces_x[k].reshape(-1, nz), t).reshape(comps, sy, nz)
        face = faces_y[k].reshape(comps * cx, 1, 1, nz)
        faces_y[k] = recv_y[k] + jnp.concatenate([face, face], axis=1).reshape(comps * sx, 1, nz)
    smooth(add_faces(r0[...], faces_x, faces_y, 1.0), r0, w, ids0, nz // 2, damping, block_in, block_out)
    out[...] = permute((x0[...] + r0[...]).reshape(-1, nz), from_lanes).reshape(out.shape)


def solution(mesh):
    axes = ("gx", "gy")
    sizes = tuple(mesh.shape[a] for a in axes)

    def per_device(source, cell_class, class_conductivity, layer_of_depth, inverses):
        comps, sx, sy, nz = source.shape
        layers, size, _ = inverses.shape
        cx, cy = sx // 2, sy // 2
        vmem = pl.BlockSpec(memory_space=pltpu.VMEM)
        hbm = pl.BlockSpec(memory_space=pltpu.HBM)
        fine, coarse = (comps, sx, sy, nz), (comps, cx, cy, nz)
        scratch = [
            ((sx // 4 * (sy // 8), size, nz), f32), ((sx // 4 * (sy // 8), size, nz), f32),
            ((2 * size, layers * size), bf16), (fine, f32), (fine, f32), (fine, f32), ((sx, sy, nz), f32), ((cx, cy, nz), f32),
            (coarse, f32), (coarse, f32), (coarse, f32), (coarse, f32), ((comps * cx * sy, nz), f32),
        ]
        scratch += [((2, comps, sy, nz), f32)] * 2 + [((2, comps * sx, 1, nz), f32)] * 2
        scratch += [((3, 2, comps // 2, cy, nz), f32)] * 2 + [((3, 2, comps * cx // 2, 1, nz), f32)] * 2
        return pl.pallas_call(
            functools.partial(kernel, axes, sizes),
            out_shape=jax.ShapeDtypeStruct(source.shape, f32),
            in_specs=[hbm] * 5,
            out_specs=vmem,
            scratch_shapes=[pltpu.VMEM(source.shape, f32), pltpu.VMEM(cell_class.shape, jnp.int32)]
            + [pltpu.SMEM(class_conductivity.shape, f32), pltpu.SMEM(layer_of_depth.shape, jnp.int32)]
            + [pltpu.VMEM(inverses.shape, f32), pltpu.SemaphoreType.DMA((5,))]
            + [pltpu.VMEM(s, t) for s, t in scratch]
            + [pltpu.SemaphoreType.DMA((4, 4)), pltpu.SemaphoreType.DMA((4, 4))],
            compiler_params=pltpu.CompilerParams(
                collective_id=0, has_side_effects=True, vmem_limit_bytes=64 * 2**20
            ),
        )(source, cell_class, class_conductivity, layer_of_depth, inverses)

    return jax.shard_map(
        per_device,
        mesh=mesh,
        in_specs=(P(None, "gx", "gy", None), P("gx", "gy", None), P(), P(), P()),
        out_specs=P(None, "gx", "gy", None),
        check_vma=False,
    )
```

```python
import functools

import jax
import jax.numpy as jnp
from jax import lax
from jax.experimental import pallas as pl
from jax.experimental.pallas import tpu as pltpu
from jax.sharding import PartitionSpec as P

damping = 0.8
MESH = pl.DeviceIdType.MESH
f32 = jnp.float32
bf16 = jnp.bfloat16


def roll(x, shift, axis):
    shift = shift % x.shape[axis]
    return x if shift == 0 else pltpu.roll(x, shift, axis)


def iota(shape, axis):
    return lax.broadcasted_iota(jnp.int32, shape, axis)


def split(x):
    hi = x.astype(bf16)
    return hi, (x - hi.astype(f32)).astype(bf16)


def dot(a, b):
    return jnp.dot(a, b, preferred_element_type=f32)


def permute(x, matrix):
    hi, lo = split(x)
    return dot(hi, matrix) + dot(lo, matrix)


def pair_rows(x, t):
    n = x.shape[0]
    t[:n, :] = x
    return t[pl.ds(0, n // 2, stride=2), :] + t[pl.ds(1, n // 2, stride=2), :]


def repeat_rows(x, t):
    n = x.shape[0]
    t[pl.ds(0, n, stride=2), :] = x
    t[pl.ds(1, n, stride=2), :] = x
    return t[: 2 * n, :]


def pack(x):
    n = x.shape[0] // 2
    return jnp.where(iota((n,) + x.shape[1:], x.ndim - 1) < x.shape[-1] // 2, x[:n], x[n:])


def unpack(x):
    half = x.shape[-1] // 2
    turned = roll(x, half, x.ndim - 1)
    first = iota(x.shape, x.ndim - 1) < half
    return jnp.concatenate([jnp.where(first, x, turned), jnp.where(first, turned, x)], axis=0)


def first_half(shape, half):
    lane = iota(shape, len(shape) - 1)
    mask = lane < half
    for start in range(2 * half, shape[-1], 2 * half):
        mask = mask | ((lane >= start) & (lane < start + half))
    return mask


def swap_tiles(v0, v1):
    low = iota(v0.shape, 1) < 4
    return jnp.where(low, v0, roll(v1, 4, 1)), jnp.where(low, roll(v0, 4, 1), v1)


def swap_lanes(a, b, half):
    mask = first_half(a.shape, half)
    return jnp.where(mask, a, roll(b, half, 1)), jnp.where(mask, roll(a, -half, 1), b)


def masked(x, ids, layers):
    tiles = x.reshape(-1, 16, x.shape[1])
    out = []
    for layer in range(layers):
        mask = jnp.broadcast_to(jnp.where(ids == layer, 1.0, 0.0), (16, x.shape[1])).astype(bf16)
        out.append((tiles * mask[None]).reshape(x.shape))
    return jnp.concatenate(out, axis=0)


def smooth(field, out_ref, w, ids, half, scale, block_in, block_out):
    comps, sx, sy, nz = field.shape
    rows = comps * 16
    size = 2 * rows
    layers = w.shape[1] // size
    pairs = [(xb, p) for xb in range(sx // 4) for p in range(sy // 8)]
    for at, (xb, p) in enumerate(pairs):
        v = field[:, 4 * xb : 4 * xb + 4, 8 * p : 8 * p + 8, :].reshape(comps * 2, 2, 8, nz)
        u0, u1 = swap_tiles(v[:, 0], v[:, 1])
        even, odd = swap_lanes(u0.reshape(rows, nz), u1.reshape(rows, nz), half)
        block_in[at, pl.ds(0, rows, stride=2), :] = even
        block_in[at, pl.ds(1, rows, stride=2), :] = odd
    n = len(pairs) * nz
    hi, lo = split(jnp.concatenate([block_in[at] for at in range(len(pairs))], axis=1))
    ids = jnp.concatenate([ids] * len(pairs), axis=1)
    if n < 256:
        x = masked(jnp.concatenate([hi, lo], axis=1), jnp.concatenate([ids, ids], axis=1), layers)
        total = dot(w[...], x)
        total = total[:size] + total[size:]
        total = total[:, :n] + total[:, n:]
    else:
        total = dot(w[...], masked(hi, ids, layers))
        total = total[:size] + total[size:] + dot(w[:size, :], masked(lo, ids, layers))
    total = total * scale
    for at, (xb, p) in enumerate(pairs):
        block_out[at] = total[:, at * nz : (at + 1) * nz]
        even = block_out[at, pl.ds(0, rows, stride=2), :]
        odd = block_out[at, pl.ds(1, rows, stride=2), :]
        u0, u1 = swap_lanes(even, odd, half)
        v0, v1 = swap_tiles(u0.reshape(comps * 2, 8, nz), u1.reshape(comps * 2, 8, nz))
        v = jnp.stack([v0, v1], axis=1).reshape(comps, 4, 8, nz)
        out_ref[:, 4 * xb : 4 * xb + 4, 8 * p : 8 * p + 8, :] = v


def residual(b, u, sigma, beside_z, factor):
    comps, sx, sy, nz = u.shape
    half = comps // 2
    flat = u.reshape(comps * sx, sy, nz)
    row = iota(flat.shape, 1)
    near = jnp.where(row == 0, 0.0, roll(flat, 1, 1)) + jnp.where(row == sy - 1, 0.0, roll(flat, -1, 1))
    near = near.reshape(u.shape) + permute(flat.reshape(-1, nz), beside_z).reshape(u.shape)
    zero = jnp.zeros((comps, 1, sy, nz), f32)
    near = near + jnp.concatenate([zero, u[:, :-1]], axis=1) + jnp.concatenate([u[:, 1:], zero], axis=1)
    out = b - (6.0 * u - near) * factor
    turned = jnp.concatenate([sigma[None] * u[half:], -(sigma[None] * u[:half])], axis=0)
    return out + turned


def add_faces(r, faces_x, faces_y, factor):
    comps, sx, sy, nz = r.shape
    row = iota((comps * sx, sy, nz), 1)
    flat = r.reshape(comps * sx, sy, nz)
    flat = flat + jnp.where(row == 0, faces_y[0] * factor, 0.0) + jnp.where(row == sy - 1, faces_y[1] * factor, 0.0)
    r = flat.reshape(r.shape)
    low = r[:, :1] + faces_x[0][:, None] * factor
    high = r[:, sx - 1 :] + faces_x[1][:, None] * factor
    return jnp.concatenate([low, r[:, 1 : sx - 1], high], axis=1)


def restrict(u, t):
    comps, sx, sy, nz = u.shape
    v = u.reshape(comps * sx // 2, 2, sy, nz)
    v = pair_rows((v[:, 0] + v[:, 1]).reshape(-1, nz), t)
    v = (v + roll(v, nz // 2, 1)) * 0.125
    return v.reshape(comps, sx // 2, sy // 2, nz)


def kernel(
    axes, sizes, src_hbm, cls_hbm, cond_hbm, depth_hbm, inv_hbm, out,
    src, cls, cond, depth, inv, in_sem, block_in, block_out, w, b0, x0, r0, sig0, sig1, b1, x1, r1, d1, t,
    send_x, recv_x, send_y, recv_y, csend_x, crecv_x, csend_y, crecv_y, send_sem, recv_sem,
):
    comps, sx, sy, nz = src.shape
    named = ((src_hbm, src), (cls_hbm, cls), (cond_hbm, cond), (depth_hbm, depth), (inv_hbm, inv))
    loads = [pltpu.make_async_copy(a, b, in_sem.at[i]) for i, (a, b) in enumerate(named)]
    for load in loads:
        load.start()
    me = [lax.axis_index(a) for a in axes]
    has = [me[0] > 0, me[0] < sizes[0] - 1, me[1] > 0, me[1] < sizes[1] - 1]

    def device(d):
        n = sizes[d // 2]
        return {axes[d // 2]: lax.rem(me[d // 2] + (n - 1 if d % 2 == 0 else 1), n)}

    barrier = pltpu.get_barrier_semaphore()
    for d in range(4):
        @pl.when(has[d])
        def _(d=d):
            pl.semaphore_signal(barrier, inc=1, device_id=device(d), device_id_type=MESH)

        @pl.when(jnp.logical_not(has[d]))
        def _(d=d):
            for ref in [(recv_x, crecv_x), (recv_y, crecv_y)][d // 2]:
                if ref is recv_x or ref is recv_y:
                    ref[d % 2] = jnp.zeros(ref.shape[1:], f32)
                else:
                    for e in range(3):
                        ref[e, d % 2] = jnp.zeros(ref.shape[2:], f32)

    def copy(e, d):
        if d < 2:
            s, r = (send_x, recv_x) if e == 3 else (csend_x.at[e], crecv_x.at[e])
        else:
            s, r = (send_y, recv_y) if e == 3 else (csend_y.at[e], crecv_y.at[e])
        k = d % 2
        return pltpu.make_async_remote_copy(
            src_ref=s.at[k], dst_ref=r.at[1 - k], send_sem=send_sem.at[e, d], recv_sem=recv_sem.at[e, d ^ 1],
            device_id=device(d), device_id_type=MESH,
        )

    def launch(e, directions=range(4)):
        for d in directions:
            @pl.when(has[d])
            def _(d=d):
                copy(e, d).start()

    def start(e, u):
        c, ux, uy, _ = u.shape
        flat = u.reshape(c * ux, uy, nz)
        for k in range(2):
            csend_x[e, k] = pack(u[:, k * (ux - 1)])
        launch(e, (0, 1))
        for k in range(2):
            csend_y[e, k] = pack(flat[:, k * (uy - 1) : k * (uy - 1) + 1])
        launch(e, (2, 3))

    def faces(e):
        return [unpack(crecv_x[e, k]) for k in range(2)], [unpack(crecv_y[e, k]) for k in range(2)]

    def finish(e):
        for d in range(4):
            @pl.when(has[d])
            def _(d=d):
                copy(e, d ^ 1).wait_recv()

    q = nz // 4
    def z_of(lane):
        zi = jnp.where(lane >= 2 * q, 1, 0)
        rest = lane - 2 * q * zi
        zic = jnp.where(rest >= q, 1, 0)
        return 4 * (rest - q * zic) + 2 * zic + zi
    to_lanes = jnp.where(iota((nz, nz), 0) == z_of(iota((nz, nz), 1)), 1.0, 0.0).astype(bf16)
    from_lanes = jnp.where(iota((nz, nz), 1) == z_of(iota((nz, nz), 0)), 1.0, 0.0).astype(bf16)

    beside0 = jnp.where(jnp.abs(z_of(iota((nz, nz), 0)) - z_of(iota((nz, nz), 1))) == 1, 1.0, 0.0).astype(bf16)
    def zc_of(lane):
        return z_of(lane - jnp.where(lane >= 2 * q, 2 * q, 0)) // 2
    near1 = jnp.abs(zc_of(iota((nz, nz), 0)) - zc_of(iota((nz, nz), 1))) == 1
    beside1 = jnp.where(near1 & (iota((nz, nz), 0) < 2 * q), 1.0, 0.0).astype(bf16)

    loads[0].wait()
    b0[...] = permute(src[...].reshape(-1, nz), to_lanes).reshape(src.shape)

    loads[3].wait()
    lane = iota((1, nz), 1)
    zb = zc_of(lane)
    ids0 = jnp.zeros((1, nz), jnp.int32)
    for k in range(depth.shape[0]):
        ids0 = jnp.where(zb == k, depth[k], ids0)
    ids1 = jnp.where(first_half((1, nz), q), ids0, roll(ids0, q, 1))

    loads[4].wait()
    layers, size, _ = inv.shape
    hi, lo = split(jnp.concatenate([inv[layer] for layer in range(layers)], axis=1))
    w[:size, :] = hi
    w[size:, :] = lo

    smooth(b0[...], x0, w, ids0, nz // 2, damping, block_in, block_out)
    pl.semaphore_wait(barrier, sum(jnp.where(h, 1, 0) for h in has))
    flat = x0[...].reshape(comps * sx, sy, nz)
    for k in range(2):
        face = x0[:, k * (sx - 1)]
        face = pair_rows(face.reshape(comps * sy, nz), t).reshape(comps, sy // 2, nz)
        csend_x[0, k] = pack((face + roll(face, nz // 2, 2)) * 0.125)
    launch(0, (0, 1))
    for k in range(2):
        send_y[k] = flat[:, k * (sy - 1) : k * (sy - 1) + 1]
        face = send_y[k].reshape(comps * sx // 2, 2, 1, nz)
        face = face[:, 0] + face[:, 1]
        csend_y[0, k] = pack((face + roll(face, nz // 2, 2)) * 0.125)
    launch(0, (2, 3))

    loads[1].wait()
    kinds = dot(cls[...].reshape(-1, nz).astype(f32).astype(bf16), to_lanes)
    loads[2].wait()
    sigma = jnp.zeros_like(kinds)
    for k in range(cond.shape[0]):
        sigma = jnp.where(kinds == float(k), cond[k], sigma)
    sigma = sigma.reshape(sx, sy, nz)
    sig0[...] = sigma
    sig1[...] = restrict(sigma[None], t)[0]

    r0[...] = residual(b0[...], x0[...], sig0[...], beside0, 1.0)
    for k in range(2):
        send_x[k] = x0[:, k * (sx - 1)]
    launch(3)
    b1[...] = restrict(r0[...], t)
    finish(0)
    b1[...] = add_faces(b1[...], *faces(0), 1.0)

    smooth(b1[...], x1, w, ids1, q, damping * 4.0, block_in, block_out)
    start(1, x1[...])
    r1[...] = residual(b1[...], x1[...], sig1[...], beside1, 0.25)
    finish(1)
    smooth(add_faces(r1[...], *faces(1), 0.25), d1, w, ids1, q, damping * 4.0, block_in, block_out)
    xc = x1[...] + d1[...]
    start(2, xc)
    cx, cy = sx // 2, sy // 2
    spread = repeat_rows(xc.reshape(-1, nz), t).reshape(comps, cx, 1, sy, nz)
    spread = jnp.concatenate([spread, spread], axis=2).reshape(src.shape)
    x0[...] = x0[...] + spread
    r0[...] = residual(b0[...], x0[...], sig0[...], beside0, 1.0)
    finish(3)
    finish(2)
    faces_x, faces_y = faces(2)
    for k in range(2):
        faces_x[k] = recv_x[k] + repeat_rows(faces_x[k].reshape(-1, nz), t).reshape(comps, sy, nz)
        face = faces_y[k].reshape(comps * cx, 1, 1, nz)
        faces_y[k] = recv_y[k] + jnp.concatenate([face, face], axis=1).reshape(comps * sx, 1, nz)
    smooth(add_faces(r0[...], faces_x, faces_y, 1.0), r0, w, ids0, nz // 2, damping, block_in, block_out)
    out[...] = permute((x0[...] + r0[...]).reshape(-1, nz), from_lanes).reshape(out.shape)
    for e in range(4):
        for d in range(4):
            @pl.when(has[d])
            def _(e=e, d=d):
                copy(e, d).wait_send()


def solution(mesh):
    axes = ("gx", "gy")
    sizes = tuple(mesh.shape[a] for a in axes)

    def per_device(source, cell_class, class_conductivity, layer_of_depth, inverses):
        operands = (source, cell_class, class_conductivity, layer_of_depth, inverses)
        comps, sx, sy, nz = source.shape
        layers, size, _ = inverses.shape
        cx, cy = sx // 2, sy // 2
        vmem = pl.BlockSpec(memory_space=pltpu.VMEM)
        hbm = pl.BlockSpec(memory_space=pltpu.HBM)
        fine, coarse = (comps, sx, sy, nz), (comps, cx, cy, nz)
        scratch = [
            ((sx // 4 * (sy // 8), size, nz), f32), ((sx // 4 * (sy // 8), size, nz), f32),
            ((2 * size, layers * size), bf16), (fine, f32), (fine, f32), (fine, f32), ((sx, sy, nz), f32), ((cx, cy, nz), f32),
            (coarse, f32), (coarse, f32), (coarse, f32), (coarse, f32), ((comps * cx * sy, nz), f32),
        ]
        scratch += [((2, comps, sy, nz), f32)] * 2 + [((2, comps * sx, 1, nz), f32)] * 2
        scratch += [((3, 2, comps // 2, cy, nz), f32)] * 2 + [((3, 2, comps * cx // 2, 1, nz), f32)] * 2
        return pl.pallas_call(
            functools.partial(kernel, axes, sizes),
            out_shape=jax.ShapeDtypeStruct(source.shape, f32),
            in_specs=[hbm] * 5,
            out_specs=vmem,
            scratch_shapes=[pltpu.VMEM(source.shape, f32), pltpu.VMEM(cell_class.shape, jnp.int32)]
            + [pltpu.SMEM(class_conductivity.shape, f32), pltpu.SMEM(layer_of_depth.shape, jnp.int32)]
            + [pltpu.VMEM(inverses.shape, f32), pltpu.SemaphoreType.DMA((5,))]
            + [pltpu.VMEM(s, t) for s, t in scratch]
            + [pltpu.SemaphoreType.DMA((4, 4)), pltpu.SemaphoreType.DMA((4, 4))],
            compiler_params=pltpu.CompilerParams(
                collective_id=0, has_side_effects=True, vmem_limit_bytes=50 * 2**20
            ),
        )(*(pltpu.with_memory_space_constraint(v, pltpu.HBM) for v in operands))

    return jax.shard_map(
        per_device,
        mesh=mesh,
        in_specs=(P(None, "gx", "gy", None), P("gx", "gy", None), P(), P(), P()),
        out_specs=P(None, "gx", "gy", None),
        check_vma=False,
    )
```

```python
import functools

import jax
import jax.numpy as jnp
from jax import lax
from jax.experimental import pallas as pl
from jax.experimental.pallas import tpu as pltpu
from jax.sharding import PartitionSpec as P

damping = 0.8
MESH = pl.DeviceIdType.MESH
f32 = jnp.float32
bf16 = jnp.bfloat16


def roll(x, shift, axis):
    shift = shift % x.shape[axis]
    return x if shift == 0 else pltpu.roll(x, shift, axis)


def iota(shape, axis):
    return lax.broadcasted_iota(jnp.int32, shape, axis)


def split(x):
    hi = x.astype(bf16)
    return hi, (x - hi.astype(f32)).astype(bf16)


def dot(a, b):
    return jnp.dot(a, b, preferred_element_type=f32)


def permute(x, matrix):
    hi, lo = split(x)
    return dot(hi, matrix) + dot(lo, matrix)


def pair_rows(x, t):
    n = x.shape[0]
    t[:n, :] = x
    return t[pl.ds(0, n // 2, stride=2), :] + t[pl.ds(1, n // 2, stride=2), :]


def repeat_rows(x, t):
    n = x.shape[0]
    t[pl.ds(0, n, stride=2), :] = x
    t[pl.ds(1, n, stride=2), :] = x
    return t[: 2 * n, :]


def pack(x):
    n = x.shape[0] // 2
    return jnp.where(iota((n,) + x.shape[1:], x.ndim - 1) < x.shape[-1] // 2, x[:n], x[n:])


def unpack(x):
    half = x.shape[-1] // 2
    turned = roll(x, half, x.ndim - 1)
    first = iota(x.shape, x.ndim - 1) < half
    return jnp.concatenate([jnp.where(first, x, turned), jnp.where(first, turned, x)], axis=0)


def first_half(shape, half):
    lane = iota(shape, len(shape) - 1)
    mask = lane < half
    for start in range(2 * half, shape[-1], 2 * half):
        mask = mask | ((lane >= start) & (lane < start + half))
    return mask


def swap_tiles(v0, v1):
    low = iota(v0.shape, 1) < 4
    return jnp.where(low, v0, roll(v1, 4, 1)), jnp.where(low, roll(v0, 4, 1), v1)


def swap_lanes(a, b, half):
    mask = first_half(a.shape, half)
    return jnp.where(mask, a, roll(b, half, 1)), jnp.where(mask, roll(a, -half, 1), b)


def masked(x, ids, layers):
    tiles = x.reshape(-1, 16, x.shape[1])
    out = []
    for layer in range(layers):
        mask = jnp.broadcast_to(jnp.where(ids == layer, 1.0, 0.0), (16, x.shape[1])).astype(bf16)
        out.append((tiles * mask[None]).reshape(x.shape))
    return jnp.concatenate(out, axis=0)


def smooth(field, out_ref, w, ids, half, scale, block_in, block_out, mix_in=None, mix_out=None):
    comps, sx, sy, nz = field.shape
    rows = comps * 16
    size = 2 * rows
    layers = w.shape[1] // size
    pairs = [(xb, p) for xb in range(sx // 4) for p in range(sy // 8)]
    for at, (xb, p) in enumerate(pairs):
        v = field[:, 4 * xb : 4 * xb + 4, 8 * p : 8 * p + 8, :].reshape(comps * 2, 2, 8, nz)
        u0, u1 = swap_tiles(v[:, 0], v[:, 1])
        u0, u1 = u0.reshape(rows, nz), u1.reshape(rows, nz)
        if mix_in is None:
            even, odd = swap_lanes(u0, u1, half)
        else:
            mixed = permute(jnp.concatenate([u0, u1], axis=1), mix_in)
            even, odd = mixed[:, :nz], mixed[:, nz:]
        block_in[at, pl.ds(0, rows, stride=2), :] = even
        block_in[at, pl.ds(1, rows, stride=2), :] = odd
    n = len(pairs) * nz
    hi, lo = split(jnp.concatenate([block_in[at] for at in range(len(pairs))], axis=1))
    ids = jnp.concatenate([ids] * len(pairs), axis=1)
    if n < 256:
        x = masked(jnp.concatenate([hi, lo], axis=1), jnp.concatenate([ids, ids], axis=1), layers)
        total = dot(w[...], x)
        total = total[:size] + total[size:]
        total = total[:, :n] + total[:, n:]
    else:
        total = dot(w[...], masked(hi, ids, layers))
        total = total[:size] + total[size:] + dot(w[:size, :], masked(lo, ids, layers))
    total = total * scale
    for at, (xb, p) in enumerate(pairs):
        block_out[at] = total[:, at * nz : (at + 1) * nz]
        even = block_out[at, pl.ds(0, rows, stride=2), :]
        odd = block_out[at, pl.ds(1, rows, stride=2), :]
        if mix_out is None:
            u0, u1 = swap_lanes(even, odd, half)
        else:
            mixed = permute(jnp.concatenate([even, odd], axis=1), mix_out)
            u0, u1 = mixed[:, :nz], mixed[:, nz:]
        v0, v1 = swap_tiles(u0.reshape(comps * 2, 8, nz), u1.reshape(comps * 2, 8, nz))
        v = jnp.stack([v0, v1], axis=1).reshape(comps, 4, 8, nz)
        at = (slice(None), slice(4 * xb, 4 * xb + 4), slice(8 * p, 8 * p + 8), slice(None))
        out_ref[at] = v if mix_out is None else out_ref[at] + v


def residual(b, u, sigma, beside_z, factor):
    comps, sx, sy, nz = u.shape
    half = comps // 2
    flat = u.reshape(comps * sx, sy, nz)
    row = iota(flat.shape, 1)
    near = jnp.where(row == 0, 0.0, roll(flat, 1, 1)) + jnp.where(row == sy - 1, 0.0, roll(flat, -1, 1))
    near = near.reshape(u.shape) + permute(flat.reshape(-1, nz), beside_z).reshape(u.shape)
    zero = jnp.zeros((comps, 1, sy, nz), f32)
    near = near + jnp.concatenate([zero, u[:, :-1]], axis=1) + jnp.concatenate([u[:, 1:], zero], axis=1)
    out = b - (6.0 * u - near) * factor
    turned = jnp.concatenate([sigma[None] * u[half:], -(sigma[None] * u[:half])], axis=0)
    return out + turned


def add_faces(r, faces_x, faces_y, factor):
    comps, sx, sy, nz = r.shape
    row = iota((comps * sx, sy, nz), 1)
    flat = r.reshape(comps * sx, sy, nz)
    flat = flat + jnp.where(row == 0, faces_y[0] * factor, 0.0) + jnp.where(row == sy - 1, faces_y[1] * factor, 0.0)
    r = flat.reshape(r.shape)
    low = r[:, :1] + faces_x[0][:, None] * factor
    high = r[:, sx - 1 :] + faces_x[1][:, None] * factor
    return jnp.concatenate([low, r[:, 1 : sx - 1], high], axis=1)


def restrict(u, t):
    comps, sx, sy, nz = u.shape
    v = u.reshape(comps * sx // 2, 2, sy, nz)
    v = pair_rows((v[:, 0] + v[:, 1]).reshape(-1, nz), t)
    v = (v + roll(v, nz // 2, 1)) * 0.125
    return v.reshape(comps, sx // 2, sy // 2, nz)


def kernel(
    axes, sizes, src_hbm, cls_hbm, cond_hbm, depth_hbm, inv_hbm, out,
    src, cls, cond, depth, inv, in_sem, block_in, block_out, w, b0, x0, r0, sig0, sig1, b1, x1, r1, d1, t,
    send_x, recv_x, send_y, recv_y, csend_x, crecv_x, csend_y, crecv_y, send_sem, recv_sem,
):
    comps, sx, sy, nz = src.shape
    named = ((src_hbm, src), (cls_hbm, cls), (cond_hbm, cond), (depth_hbm, depth), (inv_hbm, inv))
    loads = [pltpu.make_async_copy(a, b, in_sem.at[i]) for i, (a, b) in enumerate(named)]
    for load in loads:
        load.start()
    me = [lax.axis_index(a) for a in axes]
    has = [me[0] > 0, me[0] < sizes[0] - 1, me[1] > 0, me[1] < sizes[1] - 1]

    def device(d):
        n = sizes[d // 2]
        return {axes[d // 2]: lax.rem(me[d // 2] + (n - 1 if d % 2 == 0 else 1), n)}

    barrier = pltpu.get_barrier_semaphore()
    for d in range(4):
        @pl.when(has[d])
        def _(d=d):
            pl.semaphore_signal(barrier, inc=1, device_id=device(d), device_id_type=MESH)

        @pl.when(jnp.logical_not(has[d]))
        def _(d=d):
            for ref in [(recv_x, crecv_x), (recv_y, crecv_y)][d // 2]:
                if ref is recv_y:
                    ref[d % 2] = jnp.zeros(ref.shape[1:], f32)
                else:
                    for e in range(ref.shape[0]):
                        ref[e, d % 2] = jnp.zeros(ref.shape[2:], f32)

    def copy(e, d):
        if d < 2:
            s, r = (send_x.at[e - 3], recv_x.at[e - 3]) if e >= 3 else (csend_x.at[e], crecv_x.at[e])
        else:
            s, r = (send_y, recv_y) if e >= 3 else (csend_y.at[e], crecv_y.at[e])
        k = d % 2
        return pltpu.make_async_remote_copy(
            src_ref=s.at[k], dst_ref=r.at[1 - k], send_sem=send_sem.at[e, d], recv_sem=recv_sem.at[e, d ^ 1],
            device_id=device(d), device_id_type=MESH,
        )

    def launch(e, directions=range(4)):
        for d in directions:
            @pl.when(has[d])
            def _(d=d):
                copy(e, d).start()

    def start(e, u):
        c, ux, uy, _ = u.shape
        flat = u.reshape(c * ux, uy, nz)
        for k in range(2):
            csend_x[e, k] = pack(u[:, k * (ux - 1)])
        launch(e, (0, 1))
        for k in range(2):
            csend_y[e, k] = pack(flat[:, k * (uy - 1) : k * (uy - 1) + 1])
        launch(e, (2, 3))

    def faces(e):
        return [unpack(crecv_x[e, k]) for k in range(2)], [unpack(crecv_y[e, k]) for k in range(2)]

    def finish(e, directions=range(4)):
        for d in directions:
            @pl.when(has[d])
            def _(d=d):
                copy(e, d ^ 1).wait_recv()

    q = nz // 4
    def z_of(lane):
        zi = jnp.where(lane >= 2 * q, 1, 0)
        rest = lane - 2 * q * zi
        zic = jnp.where(rest >= q, 1, 0)
        return 4 * (rest - q * zic) + 2 * zic + zi
    to_lanes = jnp.where(iota((nz, nz), 0) == z_of(iota((nz, nz), 1)), 1.0, 0.0).astype(bf16)
    from_lanes = jnp.where(iota((nz, nz), 1) == z_of(iota((nz, nz), 0)), 1.0, 0.0).astype(bf16)

    beside0 = jnp.where(jnp.abs(z_of(iota((nz, nz), 0)) - z_of(iota((nz, nz), 1))) == 1, 1.0, 0.0).astype(bf16)
    def zc_of(lane):
        return z_of(lane - jnp.where(lane >= 2 * q, 2 * q, 0)) // 2
    near1 = jnp.abs(zc_of(iota((nz, nz), 0)) - zc_of(iota((nz, nz), 1))) == 1
    beside1 = jnp.where(near1 & (iota((nz, nz), 0) < 2 * q), 1.0, 0.0).astype(bf16)

    for i in (0, 3, 4):
        loads[i].wait()

    lane = iota((1, nz), 1)
    zb = zc_of(lane)
    ids0 = jnp.zeros((1, nz), jnp.int32)
    for k in range(depth.shape[0]):
        ids0 = jnp.where(zb == k, depth[k], ids0)
    ids1 = jnp.where(first_half((1, nz), q), ids0, roll(ids0, q, 1))

    layers, size, _ = inv.shape
    hi, lo = split(jnp.concatenate([inv[layer] for layer in range(layers)], axis=1))
    w[:size, :] = hi
    w[size:, :] = lo

    def mix(a, b):
        side = jnp.where(b >= nz, 1, 0)
        lane = b - nz * side
        second = jnp.where(lane >= 2 * q, 1, 0)
        return jnp.where(a == nz * second + z_of(lane - 2 * q * second + 2 * q * side), 1.0, 0.0).astype(bf16)
    wide = (2 * nz, 2 * nz)
    mix_in, mix_out = mix(iota(wide, 0), iota(wide, 1)), mix(iota(wide, 1), iota(wide, 0))

    smooth(src[...], x0, w, ids0, nz // 2, damping, block_in, block_out, mix_in=mix_in)
    pl.semaphore_wait(barrier, sum(jnp.where(h, 1, 0) for h in has))
    flat = x0[...].reshape(comps * sx, sy, nz)
    for k in range(2):
        face = x0[:, k * (sx - 1)]
        face = pair_rows(face.reshape(comps * sy, nz), t).reshape(comps, sy // 2, nz)
        csend_x[0, k] = pack((face + roll(face, nz // 2, 2)) * 0.125)
    launch(0, (0, 1))
    for k in range(2):
        send_y[k] = flat[:, k * (sy - 1) : k * (sy - 1) + 1]
        face = send_y[k].reshape(comps * sx // 2, 2, 1, nz)
        face = face[:, 0] + face[:, 1]
        csend_y[0, k] = pack((face + roll(face, nz // 2, 2)) * 0.125)
    launch(0, (2, 3))

    loads[1].wait()
    kinds = dot(cls[...].reshape(-1, nz).astype(f32).astype(bf16), to_lanes)
    loads[2].wait()
    sigma = jnp.zeros_like(kinds)
    for k in range(cond.shape[0]):
        sigma = jnp.where(kinds == float(k), cond[k], sigma)
    sigma = sigma.reshape(sx, sy, nz)
    sig0[...] = sigma
    sig1[...] = restrict(sigma[None], t)[0]

    b0[...] = permute(src[...].reshape(-1, nz), to_lanes).reshape(src.shape)
    r0[...] = residual(b0[...], x0[...], sig0[...], beside0, 1.0)
    for k in range(2):
        for h in range(2):
            send_x[h, k] = x0[h * (comps // 2) : (h + 1) * (comps // 2), k * (sx - 1)]
    b1[...] = restrict(r0[...], t)
    finish(0)
    launch(3)
    b1[...] = add_faces(b1[...], *faces(0), 1.0)

    smooth(b1[...], x1, w, ids1, q, damping * 4.0, block_in, block_out)
    start(1, x1[...])
    r1[...] = residual(b1[...], x1[...], sig1[...], beside1, 0.25)
    finish(1)
    launch(4, (0, 1))
    smooth(add_faces(r1[...], *faces(1), 0.25), d1, w, ids1, q, damping * 4.0, block_in, block_out)
    xc = x1[...] + d1[...]
    start(2, xc)
    cx, cy = sx // 2, sy // 2
    spread = repeat_rows(xc.reshape(-1, nz), t).reshape(comps, cx, 1, sy, nz)
    spread = jnp.concatenate([spread, spread], axis=2).reshape(src.shape)
    x0[...] = x0[...] + spread
    r0[...] = residual(b0[...], x0[...], sig0[...], beside0, 1.0)
    out[...] = permute(x0[...].reshape(-1, nz), from_lanes).reshape(out.shape)
    finish(3)
    finish(4, (0, 1))
    finish(2)
    faces_x, faces_y = faces(2)
    for k in range(2):
        faces_x[k] = jnp.concatenate([recv_x[0, k], recv_x[1, k]], axis=0) + repeat_rows(faces_x[k].reshape(-1, nz), t).reshape(comps, sy, nz)
        face = faces_y[k].reshape(comps * cx, 1, 1, nz)
        faces_y[k] = recv_y[k] + jnp.concatenate([face, face], axis=1).reshape(comps * sx, 1, nz)
    smooth(
        add_faces(r0[...], faces_x, faces_y, 1.0), out, w, ids0, nz // 2, damping, block_in, block_out, mix_out=mix_out
    )
    for e in range(5):
        for d in range(4 if e < 4 else 2):
            @pl.when(has[d])
            def _(e=e, d=d):
                copy(e, d).wait_send()


def solution(mesh):
    axes = ("gx", "gy")
    sizes = tuple(mesh.shape[a] for a in axes)

    def per_device(source, cell_class, class_conductivity, layer_of_depth, inverses):
        operands = (source, cell_class, class_conductivity, layer_of_depth, inverses)
        comps, sx, sy, nz = source.shape
        layers, size, _ = inverses.shape
        cx, cy = sx // 2, sy // 2
        vmem = pl.BlockSpec(memory_space=pltpu.VMEM)
        hbm = pl.BlockSpec(memory_space=pltpu.HBM)
        fine, coarse = (comps, sx, sy, nz), (comps, cx, cy, nz)
        scratch = [
            ((sx // 4 * (sy // 8), size, nz), f32), ((sx // 4 * (sy // 8), size, nz), f32),
            ((2 * size, layers * size), bf16), (fine, f32), (fine, f32), (fine, f32), ((sx, sy, nz), f32), ((cx, cy, nz), f32),
            (coarse, f32), (coarse, f32), (coarse, f32), (coarse, f32), ((comps * cx * sy, nz), f32),
        ]
        scratch += [((2, 2, comps // 2, sy, nz), f32)] * 2 + [((2, comps * sx, 1, nz), f32)] * 2
        scratch += [((3, 2, comps // 2, cy, nz), f32)] * 2 + [((3, 2, comps * cx // 2, 1, nz), f32)] * 2
        return pl.pallas_call(
            functools.partial(kernel, axes, sizes),
            out_shape=jax.ShapeDtypeStruct(source.shape, f32),
            in_specs=[hbm] * 5,
            out_specs=vmem,
            scratch_shapes=[pltpu.VMEM(source.shape, f32), pltpu.VMEM(cell_class.shape, jnp.int32)]
            + [pltpu.SMEM(class_conductivity.shape, f32), pltpu.SMEM(layer_of_depth.shape, jnp.int32)]
            + [pltpu.VMEM(inverses.shape, f32), pltpu.SemaphoreType.DMA((5,))]
            + [pltpu.VMEM(s, t) for s, t in scratch]
            + [pltpu.SemaphoreType.DMA((5, 4)), pltpu.SemaphoreType.DMA((5, 4))],
            compiler_params=pltpu.CompilerParams(
                collective_id=0, has_side_effects=True, vmem_limit_bytes=50 * 2**20
            ),
        )(*(pltpu.with_memory_space_constraint(v, pltpu.HBM) for v in operands))

    return jax.shard_map(
        per_device,
        mesh=mesh,
        in_specs=(P(None, "gx", "gy", None), P("gx", "gy", None), P(), P(), P()),
        out_specs=P(None, "gx", "gy", None),
        check_vma=False,
    )
```

```python
import functools

import jax
import jax.numpy as jnp
from jax import lax
from jax.experimental import pallas as pl
from jax.experimental.pallas import tpu as pltpu
from jax.sharding import PartitionSpec as P

damping = 0.8
MESH = pl.DeviceIdType.MESH
f32 = jnp.float32
bf16 = jnp.bfloat16


def roll(x, shift, axis):
    shift = shift % x.shape[axis]
    return x if shift == 0 else pltpu.roll(x, shift, axis)


def iota(shape, axis):
    return lax.broadcasted_iota(jnp.int32, shape, axis)


def split(x):
    hi = x.astype(bf16)
    return hi, (x - hi.astype(f32)).astype(bf16)


def dot(a, b):
    return jnp.dot(a, b, preferred_element_type=f32)


def permute(x, matrix):
    hi, lo = split(x)
    return dot(hi, matrix) + dot(lo, matrix)


def pair_rows(x, t):
    n = x.shape[0]
    t[:n, :] = x
    return t[pl.ds(0, n // 2, stride=2), :] + t[pl.ds(1, n // 2, stride=2), :]


def repeat_rows(x, t):
    n = x.shape[0]
    t[pl.ds(0, n, stride=2), :] = x
    t[pl.ds(1, n, stride=2), :] = x
    return t[: 2 * n, :]


def pack(x):
    n = x.shape[0] // 2
    return jnp.where(iota((n,) + x.shape[1:], x.ndim - 1) < x.shape[-1] // 2, x[:n], x[n:])


def unpack(x):
    half = x.shape[-1] // 2
    turned = roll(x, half, x.ndim - 1)
    first = iota(x.shape, x.ndim - 1) < half
    return jnp.concatenate([jnp.where(first, x, turned), jnp.where(first, turned, x)], axis=0)


def first_half(shape, half):
    lane = iota(shape, len(shape) - 1)
    mask = lane < half
    for start in range(2 * half, shape[-1], 2 * half):
        mask = mask | ((lane >= start) & (lane < start + half))
    return mask


def swap_tiles(v0, v1):
    low = iota(v0.shape, 1) < 4
    return jnp.where(low, v0, roll(v1, 4, 1)), jnp.where(low, roll(v0, 4, 1), v1)


def swap_lanes(a, b, half):
    mask = first_half(a.shape, half)
    return jnp.where(mask, a, roll(b, half, 1)), jnp.where(mask, roll(a, -half, 1), b)


def masked(x, ids, layers):
    tiles = x.reshape(-1, 16, x.shape[1])
    out = []
    for layer in range(layers):
        mask = jnp.broadcast_to(jnp.where(ids == layer, 1.0, 0.0), (16, x.shape[1])).astype(bf16)
        out.append((tiles * mask[None]).reshape(x.shape))
    return jnp.concatenate(out, axis=0)


def smooth(field, out_ref, w, ids, half, scale, block_in, block_out, mix_in=None, mix_out=None):
    comps, sx, sy, nz = field.shape
    rows = comps * 16
    size = 2 * rows
    layers = w.shape[1] // size
    pairs = [(xb, p) for xb in range(sx // 4) for p in range(sy // 8)]
    for at, (xb, p) in enumerate(pairs):
        v = field[:, 4 * xb : 4 * xb + 4, 8 * p : 8 * p + 8, :].reshape(comps * 2, 2, 8, nz)
        u0, u1 = swap_tiles(v[:, 0], v[:, 1])
        u0, u1 = u0.reshape(rows, nz), u1.reshape(rows, nz)
        if mix_in is None:
            even, odd = swap_lanes(u0, u1, half)
        else:
            mixed = permute(jnp.concatenate([u0, u1], axis=1), mix_in)
            even, odd = mixed[:, :nz], mixed[:, nz:]
        block_in[at, pl.ds(0, rows, stride=2), :] = even
        block_in[at, pl.ds(1, rows, stride=2), :] = odd
    x = jnp.concatenate([block_in[at, :size, :] for at in range(len(pairs))], axis=1)
    hi, lo = split(x)
    ids = jnp.concatenate([ids] * len(pairs), axis=1)
    twice = half < nz // 2
    if twice:
        x = jnp.where(first_half(x.shape, nz // 2), hi.astype(f32), x - hi.astype(f32)).astype(bf16)
        total = dot(w[...], masked(x, ids, layers))
        total = total[:size] + total[size:]
    else:
        total = dot(w[...], masked(hi, ids, layers))
        total = total[:size] + total[size:] + dot(w[:size, :], masked(lo, ids, layers))
    total = total * scale
    for at, (xb, p) in enumerate(pairs):
        block = total[:, at * nz : (at + 1) * nz]
        block_out[at, :size, :] = block + roll(block, nz // 2, 1) if twice else block
        even = block_out[at, pl.ds(0, rows, stride=2), :]
        odd = block_out[at, pl.ds(1, rows, stride=2), :]
        if mix_out is None:
            u0, u1 = swap_lanes(even, odd, half)
        else:
            mixed = permute(jnp.concatenate([even, odd], axis=1), mix_out)
            u0, u1 = mixed[:, :nz], mixed[:, nz:]
        v0, v1 = swap_tiles(u0.reshape(comps * 2, 8, nz), u1.reshape(comps * 2, 8, nz))
        v = jnp.stack([v0, v1], axis=1).reshape(comps, 4, 8, nz)
        if mix_out is None:
            for c in range(comps):
                for i in range(4):
                    out_ref[pl.ds((c * sx + 4 * xb + i) * sy + 8 * p, 8), :] = v[c, i]
        else:
            at = (slice(None), slice(4 * xb, 4 * xb + 4), slice(8 * p, 8 * p + 8), slice(None))
            out_ref[at] = out_ref[at] + v


def residual(b, u, sigma, beside_z, factor):
    comps, sx, sy, nz = u.shape
    half = comps // 2
    flat = u.reshape(comps * sx, sy, nz)
    row = iota(flat.shape, 1)
    near = jnp.where(row == 0, 0.0, roll(flat, 1, 1)) + jnp.where(row == sy - 1, 0.0, roll(flat, -1, 1))
    near = near.reshape(u.shape) + permute(flat.reshape(-1, nz), beside_z).reshape(u.shape)
    zero = jnp.zeros((comps, 1, sy, nz), f32)
    near = near + jnp.concatenate([zero, u[:, :-1]], axis=1) + jnp.concatenate([u[:, 1:], zero], axis=1)
    out = b - (6.0 * u - near) * factor
    turned = jnp.concatenate([sigma[None] * u[half:], -(sigma[None] * u[:half])], axis=0)
    return out + turned


def add_faces(r, shape, faces_x, faces_y):
    comps, sx, sy, nz = shape
    for k in range(2):
        for c in range(comps):
            at = pl.ds((c * sx + k * (sx - 1)) * sy, sy)
            r[at, :] = r[at, :] + faces_x[k][c]
        at = pl.ds(k * (sy - 1), comps * sx, stride=sy)
        r[at, :] = r[at, :] + faces_y[k]


def restrict(u, t):
    comps, sx, sy, nz = u.shape
    v = u.reshape(comps * sx // 2, 2, sy, nz)
    v = pair_rows((v[:, 0] + v[:, 1]).reshape(-1, nz), t)
    v = (v + roll(v, nz // 2, 1)) * 0.125
    return v.reshape(comps, sx // 2, sy // 2, nz)


def kernel(
    axes, sizes, src_hbm, cls_hbm, cond_hbm, depth_hbm, inv_hbm, out,
    src, cls, cond, depth, inv, in_sem, block_in, block_out, w, b0, x0, r0, sig0, sig1, b1, x1, r1, d1, t,
    send_x, recv_x, send_y, recv_y, csend_x, crecv_x, csend_y, crecv_y, send_sem, recv_sem,
):
    comps, sx, sy, nz = src.shape
    named = ((src_hbm, src), (cls_hbm, cls), (cond_hbm, cond), (depth_hbm, depth))
    layers, size, _ = inv.shape
    named += tuple((inv_hbm.at[layer], inv.at[layer]) for layer in range(layers))
    loads = [pltpu.make_async_copy(a, b, in_sem.at[i]) for i, (a, b) in enumerate(named)]
    for load in loads:
        load.start()
    me = [lax.axis_index(a) for a in axes]
    has = [me[0] > 0, me[0] < sizes[0] - 1, me[1] > 0, me[1] < sizes[1] - 1]

    def device(d):
        n = sizes[d // 2]
        return {axes[d // 2]: lax.rem(me[d // 2] + (n - 1 if d % 2 == 0 else 1), n)}

    barrier = pltpu.get_barrier_semaphore()
    for d in range(4):
        @pl.when(has[d])
        def _(d=d):
            pl.semaphore_signal(barrier, inc=1, device_id=device(d), device_id_type=MESH)

        @pl.when(jnp.logical_not(has[d]))
        def _(d=d):
            for ref in [(recv_x, crecv_x), (recv_y, crecv_y)][d // 2]:
                if ref is recv_y:
                    ref[d % 2] = jnp.zeros(ref.shape[1:], f32)
                else:
                    for e in range(ref.shape[0]):
                        ref[e, d % 2] = jnp.zeros(ref.shape[2:], f32)

    def copy(e, d):
        if d < 2:
            s, r = (send_x.at[e - 3], recv_x.at[e - 3]) if e >= 3 else (csend_x.at[e], crecv_x.at[e])
        else:
            s, r = (send_y, recv_y) if e >= 3 else (csend_y.at[e], crecv_y.at[e])
        k = d % 2
        return pltpu.make_async_remote_copy(
            src_ref=s.at[k], dst_ref=r.at[1 - k], send_sem=send_sem.at[e, d], recv_sem=recv_sem.at[e, d ^ 1],
            device_id=device(d), device_id_type=MESH,
        )

    def launch(e, directions=range(4)):
        for d in directions:
            @pl.when(has[d])
            def _(d=d):
                copy(e, d).start()

    fine, coarse = src.shape, (comps, sx // 2, sy // 2, nz)
    nf, nc = comps * sx * sy, comps * (sx // 2) * (sy // 2)

    def start(e, u):
        _, ux, uy, _ = coarse
        for k in range(2):
            csend_x[e, k] = pack(u[:nc, :].reshape(coarse)[:, k * (ux - 1)])
        launch(e, (0, 1))
        for k in range(2):
            csend_y[e, k] = u[pl.ds(k * (uy - 1), comps * ux, stride=uy), :]
        launch(e, (2, 3))

    def faces(e, factor):
        return [unpack(crecv_x[e, k]) * factor for k in range(2)], [crecv_y[e, k] * factor for k in range(2)]

    def finish(e, directions=range(4)):
        for d in directions:
            @pl.when(has[d])
            def _(d=d):
                copy(e, d ^ 1).wait_recv()

    q = nz // 4
    def z_of(lane):
        zi = jnp.where(lane >= 2 * q, 1, 0)
        rest = lane - 2 * q * zi
        zic = jnp.where(rest >= q, 1, 0)
        return 4 * (rest - q * zic) + 2 * zic + zi
    to_lanes = jnp.where(iota((nz, nz), 0) == z_of(iota((nz, nz), 1)), 1.0, 0.0).astype(bf16)
    from_lanes = jnp.where(iota((nz, nz), 1) == z_of(iota((nz, nz), 0)), 1.0, 0.0).astype(bf16)

    beside0 = jnp.where(jnp.abs(z_of(iota((nz, nz), 0)) - z_of(iota((nz, nz), 1))) == 1, 1.0, 0.0).astype(bf16)
    def zc_of(lane):
        return z_of(lane - jnp.where(lane >= 2 * q, 2 * q, 0)) // 2
    near1 = jnp.abs(zc_of(iota((nz, nz), 0)) - zc_of(iota((nz, nz), 1))) == 1
    beside1 = jnp.where(near1 & (iota((nz, nz), 0) < 2 * q), 1.0, 0.0).astype(bf16)

    for i in (0, 3):
        loads[i].wait()

    lane = iota((1, nz), 1)
    zb = zc_of(lane)
    ids0 = jnp.zeros((1, nz), jnp.int32)
    for k in range(depth.shape[0]):
        ids0 = jnp.where(zb == k, depth[k], ids0)
    ids1 = jnp.where(first_half((1, nz), q), ids0, roll(ids0, q, 1))

    for layer in range(0, layers, 2):
        loads[4 + layer].wait()
        loads[5 + layer].wait()
        hi, lo = split(jnp.concatenate([inv[layer], inv[layer + 1]], axis=1))
        at = slice(layer * size, (layer + 2) * size)
        w[:size, at] = hi
        w[size:, at] = lo

    def mix(a, b):
        side = jnp.where(b >= nz, 1, 0)
        lane = b - nz * side
        second = jnp.where(lane >= 2 * q, 1, 0)
        return jnp.where(a == nz * second + z_of(lane - 2 * q * second + 2 * q * side), 1.0, 0.0).astype(bf16)
    wide = (2 * nz, 2 * nz)
    mix_in, mix_out = mix(iota(wide, 0), iota(wide, 1)), mix(iota(wide, 1), iota(wide, 0))

    smooth(src[...], x0, w, ids0, nz // 2, damping, block_in, block_out, mix_in=mix_in)
    pl.semaphore_wait(barrier, sum(jnp.where(h, 1, 0) for h in has))
    for k in range(2):
        face = x0[:nf, :].reshape(fine)[:, k * (sx - 1)]
        face = pair_rows(face.reshape(comps * sy, nz), t).reshape(comps, sy // 2, nz)
        csend_x[0, k] = pack((face + roll(face, nz // 2, 2)) * 0.125)
    launch(0, (0, 1))
    for k in range(2):
        face = x0[pl.ds(k * (sy - 1), comps * sx, stride=sy), :]
        send_y[k] = face
        face = pair_rows(face, t)
        csend_y[0, k] = (face + roll(face, nz // 2, 1)) * 0.125
    launch(0, (2, 3))

    loads[1].wait()
    kinds = dot(cls[...].reshape(-1, nz).astype(f32).astype(bf16), to_lanes)
    loads[2].wait()
    sigma = jnp.zeros_like(kinds)
    for k in range(cond.shape[0]):
        sigma = jnp.where(kinds == float(k), cond[k], sigma)
    sigma = sigma.reshape(sx, sy, nz)
    sig0[...] = sigma
    sig1[...] = restrict(sigma[None], t)[0]

    b0[...] = permute(src[...].reshape(-1, nz), to_lanes).reshape(src.shape)
    first = residual(b0[...], x0[:nf, :].reshape(fine), sig0[...], beside0, 1.0)
    for k in range(2):
        for h in range(2):
            send_x[h, k] = x0[:nf, :].reshape(fine)[h * (comps // 2) : (h + 1) * (comps // 2), k * (sx - 1)]
    b1[:nc, :] = restrict(first, t).reshape(nc, nz)
    finish(0)
    launch(3)
    add_faces(b1, coarse, *faces(0, 1.0))

    smooth(b1[:nc, :].reshape(coarse), x1, w, ids1, q, damping * 4.0, block_in, block_out)
    start(1, x1)
    r1[:nc, :] = residual(b1[:nc, :].reshape(coarse), x1[:nc, :].reshape(coarse), sig1[...], beside1, 0.25).reshape(nc, nz)
    finish(1)
    launch(4, (0, 1))
    add_faces(r1, coarse, *faces(1, 0.25))
    smooth(r1[:nc, :].reshape(coarse), d1, w, ids1, q, damping * 4.0, block_in, block_out)
    x1[:nc, :] = x1[:nc, :] + d1[:nc, :]
    start(2, x1)
    cx = sx // 2
    spread = repeat_rows(x1[:nc, :], t).reshape(comps, cx, 1, sy, nz)
    spread = jnp.concatenate([spread, spread], axis=2).reshape(nf, nz)
    x0[:nf, :] = x0[:nf, :] + spread
    r0[:nf, :] = residual(b0[...], x0[:nf, :].reshape(fine), sig0[...], beside0, 1.0).reshape(nf, nz)
    out[...] = permute(x0[:nf, :], from_lanes).reshape(fine)
    finish(3)
    finish(4, (0, 1))
    finish(2)
    faces_x, faces_y = faces(2, 1.0)
    for k in range(2):
        face = repeat_rows(faces_x[k].reshape(-1, nz), t).reshape(comps, sy, nz)
        faces_x[k] = jnp.concatenate([recv_x[0, k], recv_x[1, k]], axis=0) + face
        faces_y[k] = recv_y[k] + repeat_rows(faces_y[k], t)
    add_faces(r0, fine, faces_x, faces_y)
    smooth(r0[:nf, :].reshape(fine), out, w, ids0, nz // 2, damping, block_in, block_out, mix_out=mix_out)
    for e in range(5):
        for d in range(4 if e < 4 else 2):
            @pl.when(has[d])
            def _(e=e, d=d):
                copy(e, d).wait_send()


def solution(mesh):
    axes = ("gx", "gy")
    sizes = tuple(mesh.shape[a] for a in axes)

    def per_device(source, cell_class, class_conductivity, layer_of_depth, inverses):
        operands = (source, cell_class, class_conductivity, layer_of_depth, inverses)
        comps, sx, sy, nz = source.shape
        layers, size, _ = inverses.shape
        cx, cy = sx // 2, sy // 2
        vmem = pl.BlockSpec(memory_space=pltpu.VMEM)
        hbm = pl.BlockSpec(memory_space=pltpu.HBM)
        fine = source.shape
        scratch = [
            *[((sx // 4 * (sy // 8), size + 8, nz), f32)] * 2,
            ((2 * size, layers * size), bf16), (fine, f32), *[(((comps * sx + 1) * sy, nz), f32)] * 2, ((sx, sy, nz), f32), ((cx, cy, nz), f32),
            *[(((comps * cx + 1) * cy, nz), f32)] * 4, ((comps * cx * sy + 8, nz), f32),
        ]
        scratch += [((2, 2, comps // 2, sy, nz), f32)] * 2 + [((2, comps * sx, nz), f32)] * 2
        scratch += [((3, 2, comps // 2, cy, nz), f32)] * 2 + [((3, 2, comps * cx, nz), f32)] * 2
        return pl.pallas_call(
            functools.partial(kernel, axes, sizes),
            out_shape=jax.ShapeDtypeStruct(source.shape, f32),
            in_specs=[hbm] * 5,
            out_specs=vmem,
            scratch_shapes=[pltpu.VMEM(source.shape, f32), pltpu.VMEM(cell_class.shape, jnp.int32)]
            + [pltpu.SMEM(class_conductivity.shape, f32), pltpu.SMEM(layer_of_depth.shape, jnp.int32)]
            + [pltpu.VMEM(inverses.shape, f32), pltpu.SemaphoreType.DMA((4 + layers,))]
            + [pltpu.VMEM(s, t) for s, t in scratch]
            + [pltpu.SemaphoreType.DMA((5, 4)), pltpu.SemaphoreType.DMA((5, 4))],
            compiler_params=pltpu.CompilerParams(
                collective_id=0, has_side_effects=True, vmem_limit_bytes=50 * 2**20
            ),
        )(*(pltpu.with_memory_space_constraint(v, pltpu.HBM) for v in operands))

    return jax.shard_map(
        per_device,
        mesh=mesh,
        in_specs=(P(None, "gx", "gy", None), P("gx", "gy", None), P(), P(), P()),
        out_specs=P(None, "gx", "gy", None),
        check_vma=False,
    )
```

```python
import functools

import jax
import jax.numpy as jnp
from jax import lax
from jax.experimental import pallas as pl
from jax.experimental.pallas import tpu as pltpu
from jax.sharding import PartitionSpec as P

damping = 0.8
MESH = pl.DeviceIdType.MESH
f32 = jnp.float32
bf16 = jnp.bfloat16


def roll(x, shift, axis):
    shift = shift % x.shape[axis]
    return x if shift == 0 else pltpu.roll(x, shift, axis)


def iota(shape, axis):
    return lax.broadcasted_iota(jnp.int32, shape, axis)


def split(x):
    hi = x.astype(bf16)
    return hi, (x - hi.astype(f32)).astype(bf16)


def dot(a, b):
    return jnp.dot(a, b, preferred_element_type=f32)


def permute(x, matrix):
    hi, lo = split(x)
    return dot(hi, matrix) + dot(lo, matrix)


def pair_rows(x, t):
    n = x.shape[0]
    t[:n, :] = x
    return t[pl.ds(0, n // 2, stride=2), :] + t[pl.ds(1, n // 2, stride=2), :]


def repeat_rows(x, t):
    n = x.shape[0]
    t[pl.ds(0, n, stride=2), :] = x
    t[pl.ds(1, n, stride=2), :] = x
    return t[: 2 * n, :]


def pack(x):
    n = x.shape[0] // 2
    return jnp.where(iota((n,) + x.shape[1:], x.ndim - 1) < x.shape[-1] // 2, x[:n], x[n:])


def unpack(x):
    half = x.shape[-1] // 2
    turned = roll(x, half, x.ndim - 1)
    first = iota(x.shape, x.ndim - 1) < half
    return jnp.concatenate([jnp.where(first, x, turned), jnp.where(first, turned, x)], axis=0)


def first_half(shape, half):
    lane = iota(shape, len(shape) - 1)
    mask = lane < half
    for start in range(2 * half, shape[-1], 2 * half):
        mask = mask | ((lane >= start) & (lane < start + half))
    return mask


def swap_tiles(v0, v1):
    low = iota(v0.shape, 1) < 4
    return jnp.where(low, v0, roll(v1, 4, 1)), jnp.where(low, roll(v0, 4, 1), v1)


def swap_lanes(a, b, half):
    mask = first_half(a.shape, half)
    return jnp.where(mask, a, roll(b, half, 1)), jnp.where(mask, roll(a, -half, 1), b)


def masked(x, ids, layers):
    tiles = x.reshape(-1, 16, x.shape[1])
    out = []
    for layer in range(layers):
        mask = jnp.broadcast_to(jnp.where(ids == layer, 1.0, 0.0), (16, x.shape[1])).astype(bf16)
        out.append((tiles * mask[None]).reshape(x.shape))
    return jnp.concatenate(out, axis=0)


def smooth(field, out_ref, w, ids, half, scale, block_in, block_out, mix_in=None, mix_out=None):
    comps, sx, sy, nz = field.shape
    rows = comps * 16
    size = 2 * rows
    layers = w.shape[1] // size
    pairs = [(xb, p) for xb in range(sx // 4) for p in range(sy // 8)]
    pairs = list(enumerate(pairs))
    for start in range(0, len(pairs), 2):
        group = pairs[start : start + 2]
        for at, (xb, p) in group:
            v = field[:, 4 * xb : 4 * xb + 4, 8 * p : 8 * p + 8, :].reshape(comps * 2, 2, 8, nz)
            u0, u1 = swap_tiles(v[:, 0], v[:, 1])
            u0, u1 = u0.reshape(rows, nz), u1.reshape(rows, nz)
            if mix_in is None:
                even, odd = swap_lanes(u0, u1, half)
            else:
                mixed = permute(jnp.concatenate([u0, u1], axis=1), mix_in)
                even, odd = mixed[:, :nz], mixed[:, nz:]
            block_in[at, pl.ds(0, rows, stride=2), :] = even
            block_in[at, pl.ds(1, rows, stride=2), :] = odd
        x = jnp.concatenate([block_in[at, :size, :] for at, _ in group], axis=1)
        hi, lo = split(x)
        lane_ids = jnp.concatenate([ids] * len(group), axis=1)
        twice = half < nz // 2
        if twice:
            x = jnp.where(first_half(x.shape, nz // 2), hi.astype(f32), x - hi.astype(f32)).astype(bf16)
            total = dot(w[...], masked(x, lane_ids, layers))
            total = total[:size] + total[size:]
        else:
            total = dot(w[...], masked(hi, lane_ids, layers))
            total = total[:size] + total[size:] + dot(w[:size, :], masked(lo, lane_ids, layers))
        total = total * scale
        for at, (xb, p) in group:
            block = total[:, (at - start) * nz : (at - start + 1) * nz]
            block_out[at, :size, :] = block + roll(block, nz // 2, 1) if twice else block
            even = block_out[at, pl.ds(0, rows, stride=2), :]
            odd = block_out[at, pl.ds(1, rows, stride=2), :]
            if mix_out is None:
                u0, u1 = swap_lanes(even, odd, half)
            else:
                mixed = permute(jnp.concatenate([even, odd], axis=1), mix_out)
                u0, u1 = mixed[:, :nz], mixed[:, nz:]
            v0, v1 = swap_tiles(u0.reshape(comps * 2, 8, nz), u1.reshape(comps * 2, 8, nz))
            v = jnp.stack([v0, v1], axis=1).reshape(comps, 4, 8, nz)
            if mix_out is None:
                for c in range(comps):
                    for i in range(4):
                        out_ref[pl.ds((c * sx + 4 * xb + i) * sy + 8 * p, 8), :] = v[c, i]
            else:
                at = (slice(None), slice(4 * xb, 4 * xb + 4), slice(8 * p, 8 * p + 8), slice(None))
                out_ref[at] = out_ref[at] + v


def residual(b, u, sigma, beside_z, factor):
    comps, sx, sy, nz = u.shape
    half = comps // 2
    flat = u.reshape(comps * sx, sy, nz)
    row = iota(flat.shape, 1)
    near = jnp.where(row == 0, 0.0, roll(flat, 1, 1)) + jnp.where(row == sy - 1, 0.0, roll(flat, -1, 1))
    near = near.reshape(u.shape) + permute(flat.reshape(-1, nz), beside_z).reshape(u.shape)
    zero = jnp.zeros((comps, 1, sy, nz), f32)
    near = near + jnp.concatenate([zero, u[:, :-1]], axis=1) + jnp.concatenate([u[:, 1:], zero], axis=1)
    out = b - (6.0 * u - near) * factor
    turned = jnp.concatenate([sigma[None] * u[half:], -(sigma[None] * u[:half])], axis=0)
    return out + turned


def add_faces(r, shape, faces_x, faces_y):
    comps, sx, sy, nz = shape
    for k in range(2):
        for c in range(comps):
            at = pl.ds((c * sx + k * (sx - 1)) * sy, sy)
            r[at, :] = r[at, :] + faces_x[k][c]
        at = pl.ds(k * (sy - 1), comps * sx, stride=sy)
        r[at, :] = r[at, :] + faces_y[k]


def restrict(u, t):
    comps, sx, sy, nz = u.shape
    v = u.reshape(comps * sx // 2, 2, sy, nz)
    v = pair_rows((v[:, 0] + v[:, 1]).reshape(-1, nz), t)
    v = (v + roll(v, nz // 2, 1)) * 0.125
    return v.reshape(comps, sx // 2, sy // 2, nz)


def kernel(
    axes, sizes, src_hbm, cls_hbm, cond_hbm, depth_hbm, inv_hbm, out,
    src, cls, cond, depth, inv, in_sem, block_in, block_out, w, b0, x0, r0, sig0, sig1, b1, x1, r1, d1, t,
    send_x, recv_x, send_y, recv_y, csend_x, crecv_x, csend_y, crecv_y, send_sem, recv_sem,
):
    comps, sx, sy, nz = src.shape
    named = ((src_hbm, src), (cls_hbm, cls), (cond_hbm, cond), (depth_hbm, depth))
    layers, size, _ = inv.shape
    named += ((inv_hbm, inv),)
    loads = [pltpu.make_async_copy(a, b, in_sem.at[i]) for i, (a, b) in enumerate(named)]
    for load in loads:
        load.start()
    me = [lax.axis_index(a) for a in axes]
    has = [me[0] > 0, me[0] < sizes[0] - 1, me[1] > 0, me[1] < sizes[1] - 1]

    def device(d):
        n = sizes[d // 2]
        return {axes[d // 2]: lax.rem(me[d // 2] + (n - 1 if d % 2 == 0 else 1), n)}

    barrier = pltpu.get_barrier_semaphore()
    for d in range(4):
        @pl.when(has[d])
        def _(d=d):
            pl.semaphore_signal(barrier, inc=1, device_id=device(d), device_id_type=MESH)

        @pl.when(jnp.logical_not(has[d]))
        def _(d=d):
            for ref in [(recv_x, crecv_x), (recv_y, crecv_y)][d // 2]:
                if ref is recv_y:
                    ref[d % 2] = jnp.zeros(ref.shape[1:], f32)
                else:
                    for e in range(ref.shape[0]):
                        ref[e, d % 2] = jnp.zeros(ref.shape[2:], f32)

    def copy(e, d):
        if d < 2:
            s, r = (send_x.at[e - 3], recv_x.at[e - 3]) if e >= 3 else (csend_x.at[e], crecv_x.at[e])
        else:
            s, r = (send_y, recv_y) if e >= 3 else (csend_y.at[e], crecv_y.at[e])
        k = d % 2
        return pltpu.make_async_remote_copy(
            src_ref=s.at[k], dst_ref=r.at[1 - k], send_sem=send_sem.at[e, d], recv_sem=recv_sem.at[e, d ^ 1],
            device_id=device(d), device_id_type=MESH,
        )

    def launch(e, directions=range(4)):
        for d in directions:
            @pl.when(has[d])
            def _(d=d):
                copy(e, d).start()

    fine, coarse = src.shape, (comps, sx // 2, sy // 2, nz)
    nf, nc = comps * sx * sy, comps * (sx // 2) * (sy // 2)

    def start(e, u):
        _, ux, uy, _ = coarse
        for k in range(2):
            csend_x[e, k] = pack(u[:nc, :].reshape(coarse)[:, k * (ux - 1)])
        launch(e, (0, 1))
        for k in range(2):
            csend_y[e, k] = u[pl.ds(k * (uy - 1), comps * ux, stride=uy), :]
        launch(e, (2, 3))

    def faces(e, factor):
        return [unpack(crecv_x[e, k]) * factor for k in range(2)], [crecv_y[e, k] * factor for k in range(2)]

    def finish(e, directions=range(4)):
        for d in directions:
            @pl.when(has[d])
            def _(d=d):
                copy(e, d ^ 1).wait_recv()

    q = nz // 4
    def z_of(lane):
        zi = jnp.where(lane >= 2 * q, 1, 0)
        rest = lane - 2 * q * zi
        zic = jnp.where(rest >= q, 1, 0)
        return 4 * (rest - q * zic) + 2 * zic + zi
    to_lanes = jnp.where(iota((nz, nz), 0) == z_of(iota((nz, nz), 1)), 1.0, 0.0).astype(bf16)
    from_lanes = jnp.where(iota((nz, nz), 1) == z_of(iota((nz, nz), 0)), 1.0, 0.0).astype(bf16)

    beside0 = jnp.where(jnp.abs(z_of(iota((nz, nz), 0)) - z_of(iota((nz, nz), 1))) == 1, 1.0, 0.0).astype(bf16)
    def zc_of(lane):
        return z_of(lane - jnp.where(lane >= 2 * q, 2 * q, 0)) // 2
    near1 = jnp.abs(zc_of(iota((nz, nz), 0)) - zc_of(iota((nz, nz), 1))) == 1
    beside1 = jnp.where(near1 & (iota((nz, nz), 0) < 2 * q), 1.0, 0.0).astype(bf16)

    for i in (0, 3, 4):
        loads[i].wait()

    lane = iota((1, nz), 1)
    zb = zc_of(lane)
    ids0 = jnp.zeros((1, nz), jnp.int32)
    for k in range(depth.shape[0]):
        ids0 = jnp.where(zb == k, depth[k], ids0)
    ids1 = jnp.where(first_half((1, nz), q), ids0, roll(ids0, q, 1))

    hi, lo = split(jnp.concatenate([inv[layer] for layer in range(layers)], axis=1))
    w[:size, :] = hi
    w[size:, :] = lo

    def mix(a, b):
        side = jnp.where(b >= nz, 1, 0)
        lane = b - nz * side
        second = jnp.where(lane >= 2 * q, 1, 0)
        return jnp.where(a == nz * second + z_of(lane - 2 * q * second + 2 * q * side), 1.0, 0.0).astype(bf16)
    wide = (2 * nz, 2 * nz)
    mix_in, mix_out = mix(iota(wide, 0), iota(wide, 1)), mix(iota(wide, 1), iota(wide, 0))

    smooth(src[...], x0, w, ids0, nz // 2, damping, block_in, block_out, mix_in=mix_in)
    pl.semaphore_wait(barrier, sum(jnp.where(h, 1, 0) for h in has))
    for k in range(2):
        face = x0[:nf, :].reshape(fine)[:, k * (sx - 1)]
        face = pair_rows(face.reshape(comps * sy, nz), t).reshape(comps, sy // 2, nz)
        csend_x[0, k] = pack((face + roll(face, nz // 2, 2)) * 0.125)
    launch(0, (0, 1))
    for k in range(2):
        face = x0[pl.ds(k * (sy - 1), comps * sx, stride=sy), :]
        send_y[k] = face
        face = pair_rows(face, t)
        csend_y[0, k] = (face + roll(face, nz // 2, 1)) * 0.125
    launch(0, (2, 3))

    loads[1].wait()
    kinds = dot(cls[...].reshape(-1, nz).astype(f32).astype(bf16), to_lanes)
    loads[2].wait()
    sigma = jnp.zeros_like(kinds)
    for k in range(cond.shape[0]):
        sigma = jnp.where(kinds == float(k), cond[k], sigma)
    sigma = sigma.reshape(sx, sy, nz)
    sig0[...] = sigma
    sig1[...] = restrict(sigma[None], t)[0]

    b0[...] = permute(src[...].reshape(-1, nz), to_lanes).reshape(src.shape)
    first = residual(b0[...], x0[:nf, :].reshape(fine), sig0[...], beside0, 1.0)
    for k in range(2):
        for h in range(2):
            send_x[h, k] = x0[:nf, :].reshape(fine)[h * (comps // 2) : (h + 1) * (comps // 2), k * (sx - 1)]
    b1[:nc, :] = restrict(first, t).reshape(nc, nz)
    finish(0)
    launch(3)
    add_faces(b1, coarse, *faces(0, 1.0))

    smooth(b1[:nc, :].reshape(coarse), x1, w, ids1, q, damping * 4.0, block_in, block_out)
    start(1, x1)
    r1[:nc, :] = residual(b1[:nc, :].reshape(coarse), x1[:nc, :].reshape(coarse), sig1[...], beside1, 0.25).reshape(nc, nz)
    finish(1)
    launch(4, (0, 1))
    add_faces(r1, coarse, *faces(1, 0.25))
    smooth(r1[:nc, :].reshape(coarse), d1, w, ids1, q, damping * 4.0, block_in, block_out)
    x1[:nc, :] = x1[:nc, :] + d1[:nc, :]
    start(2, x1)
    cx = sx // 2
    spread = repeat_rows(x1[:nc, :], t).reshape(comps, cx, 1, sy, nz)
    spread = jnp.concatenate([spread, spread], axis=2).reshape(nf, nz)
    x0[:nf, :] = x0[:nf, :] + spread
    r0[:nf, :] = residual(b0[...], x0[:nf, :].reshape(fine), sig0[...], beside0, 1.0).reshape(nf, nz)
    out[...] = permute(x0[:nf, :], from_lanes).reshape(fine)
    finish(3)
    finish(4, (0, 1))
    finish(2)
    faces_x, faces_y = faces(2, 1.0)
    for k in range(2):
        face = repeat_rows(faces_x[k].reshape(-1, nz), t).reshape(comps, sy, nz)
        faces_x[k] = jnp.concatenate([recv_x[0, k], recv_x[1, k]], axis=0) + face
        faces_y[k] = recv_y[k] + repeat_rows(faces_y[k], t)
    add_faces(r0, fine, faces_x, faces_y)
    smooth(r0[:nf, :].reshape(fine), out, w, ids0, nz // 2, damping, block_in, block_out, mix_out=mix_out)
    for e in range(5):
        for d in range(4 if e < 4 else 2):
            @pl.when(has[d])
            def _(e=e, d=d):
                copy(e, d).wait_send()


def solution(mesh):
    axes = ("gx", "gy")
    sizes = tuple(mesh.shape[a] for a in axes)

    def per_device(source, cell_class, class_conductivity, layer_of_depth, inverses):
        operands = (source, cell_class, class_conductivity, layer_of_depth, inverses)
        comps, sx, sy, nz = source.shape
        layers, size, _ = inverses.shape
        cx, cy = sx // 2, sy // 2
        vmem = pl.BlockSpec(memory_space=pltpu.VMEM)
        hbm = pl.BlockSpec(memory_space=pltpu.HBM)
        fine = source.shape
        scratch = [
            *[((sx // 4 * (sy // 8), size + 8, nz), f32)] * 2,
            ((2 * size, layers * size), bf16), (fine, f32), *[(((comps * sx + 1) * sy, nz), f32)] * 2, ((sx, sy, nz), f32), ((cx, cy, nz), f32),
            *[(((comps * cx + 1) * cy, nz), f32)] * 4, ((comps * cx * sy + 8, nz), f32),
        ]
        scratch += [((2, 2, comps // 2, sy, nz), f32)] * 2 + [((2, comps * sx, nz), f32)] * 2
        scratch += [((3, 2, comps // 2, cy, nz), f32)] * 2 + [((3, 2, comps * cx, nz), f32)] * 2
        return pl.pallas_call(
            functools.partial(kernel, axes, sizes),
            out_shape=jax.ShapeDtypeStruct(source.shape, f32),
            in_specs=[hbm] * 5,
            out_specs=vmem,
            scratch_shapes=[pltpu.VMEM(source.shape, f32), pltpu.VMEM(cell_class.shape, jnp.int32)]
            + [pltpu.SMEM(class_conductivity.shape, f32), pltpu.SMEM(layer_of_depth.shape, jnp.int32)]
            + [pltpu.VMEM(inverses.shape, f32), pltpu.SemaphoreType.DMA((5,))]
            + [pltpu.VMEM(s, t) for s, t in scratch]
            + [pltpu.SemaphoreType.DMA((5, 4)), pltpu.SemaphoreType.DMA((5, 4))],
            compiler_params=pltpu.CompilerParams(
                collective_id=0, has_side_effects=True, vmem_limit_bytes=50 * 2**20
            ),
        )(*(pltpu.with_memory_space_constraint(v, pltpu.HBM) for v in operands))

    return jax.shard_map(
        per_device,
        mesh=mesh,
        in_specs=(P(None, "gx", "gy", None), P("gx", "gy", None), P(), P(), P()),
        out_specs=P(None, "gx", "gy", None),
        check_vma=False,
    )
```

```python
import functools

import jax
import jax.numpy as jnp
from jax import lax
from jax.experimental import pallas as pl
from jax.experimental.pallas import tpu as pltpu
from jax.sharding import PartitionSpec as P

damping = 0.8
MESH = pl.DeviceIdType.MESH
f32 = jnp.float32
bf16 = jnp.bfloat16


def roll(x, shift, axis):
    shift = shift % x.shape[axis]
    return x if shift == 0 else pltpu.roll(x, shift, axis)


def iota(shape, axis):
    return lax.broadcasted_iota(jnp.int32, shape, axis)


def split(x):
    hi = x.astype(bf16)
    return hi, (x - hi.astype(f32)).astype(bf16)


def dot(a, b):
    return jnp.dot(a, b, preferred_element_type=f32)


def permute(x, matrix):
    hi, lo = split(x)
    return dot(hi, matrix) + dot(lo, matrix)


def pair_rows(x, t):
    n = x.shape[0]
    t[:n, :] = x
    return t[pl.ds(0, n // 2, stride=2), :] + t[pl.ds(1, n // 2, stride=2), :]


def repeat_rows(x, t):
    n = x.shape[0]
    t[pl.ds(0, n, stride=2), :] = x
    t[pl.ds(1, n, stride=2), :] = x
    return t[: 2 * n, :]


def pack(x):
    n = x.shape[0] // 2
    return jnp.where(iota((n,) + x.shape[1:], x.ndim - 1) < x.shape[-1] // 2, x[:n], x[n:])


def unpack(x):
    half = x.shape[-1] // 2
    turned = roll(x, half, x.ndim - 1)
    first = iota(x.shape, x.ndim - 1) < half
    return jnp.concatenate([jnp.where(first, x, turned), jnp.where(first, turned, x)], axis=0)


def first_half(shape, half):
    lane = iota(shape, len(shape) - 1)
    mask = lane < half
    for start in range(2 * half, shape[-1], 2 * half):
        mask = mask | ((lane >= start) & (lane < start + half))
    return mask


def swap_tiles(v0, v1):
    low = iota(v0.shape, 1) < 4
    return jnp.where(low, v0, roll(v1, 4, 1)), jnp.where(low, roll(v0, 4, 1), v1)


def swap_lanes(a, b, half):
    mask = first_half(a.shape, half)
    return jnp.where(mask, a, roll(b, half, 1)), jnp.where(mask, roll(a, -half, 1), b)


def masked(x, ids, layers):
    tiles = x.reshape(-1, 16, x.shape[1])
    out = []
    for layer in range(layers):
        mask = jnp.broadcast_to(jnp.where(ids == layer, 1.0, 0.0), (16, x.shape[1])).astype(bf16)
        out.append((tiles * mask[None]).reshape(x.shape))
    return jnp.concatenate(out, axis=0)


def smooth(field, out_ref, w, w_row, ids, half, scale, block_in, block_out, mix_in=None, mix_out=None):
    comps, sx, sy, nz = field.shape
    rows = comps * 16
    size = 2 * rows
    layers = w.shape[1] // size
    pairs = [(xb, p) for xb in range(sx // 4) for p in range(sy // 8)]
    for at, (xb, p) in enumerate(pairs):
        v = field[:, 4 * xb : 4 * xb + 4, 8 * p : 8 * p + 8, :].reshape(comps * 2, 2, 8, nz)
        u0, u1 = swap_tiles(v[:, 0], v[:, 1])
        u0, u1 = u0.reshape(rows, nz), u1.reshape(rows, nz)
        if mix_in is None:
            even, odd = swap_lanes(u0, u1, half)
        else:
            mixed = permute(jnp.concatenate([u0, u1], axis=1), mix_in)
            even, odd = mixed[:, :nz], mixed[:, nz:]
        block_in[at, pl.ds(0, rows, stride=2), :] = even
        block_in[at, pl.ds(1, rows, stride=2), :] = odd
    n = len(pairs) * nz
    hi, lo = split(jnp.concatenate([block_in[at] for at in range(len(pairs))], axis=1))
    ids = jnp.concatenate([ids] * len(pairs), axis=1)
    if n < 256:
        x = masked(jnp.concatenate([hi, lo], axis=1), jnp.concatenate([ids, ids], axis=1), layers)
        total = dot(w[...], x)
        total = total[:size] + total[size:]
        total = total[:, :n] + total[:, n:]
    else:
        high = masked(hi, ids, layers)
        total = dot(w_row[...], jnp.concatenate([high, high, masked(lo, ids, layers)], axis=0))
    total = total * scale
    for at, (xb, p) in enumerate(pairs):
        block_out[at] = total[:, at * nz : (at + 1) * nz]
        even = block_out[at, pl.ds(0, rows, stride=2), :]
        odd = block_out[at, pl.ds(1, rows, stride=2), :]
        if mix_out is None:
            u0, u1 = swap_lanes(even, odd, half)
        else:
            mixed = permute(jnp.concatenate([even, odd], axis=1), mix_out)
            u0, u1 = mixed[:, :nz], mixed[:, nz:]
        v0, v1 = swap_tiles(u0.reshape(comps * 2, 8, nz), u1.reshape(comps * 2, 8, nz))
        v = jnp.stack([v0, v1], axis=1).reshape(comps, 4, 8, nz)
        at = (slice(None), slice(4 * xb, 4 * xb + 4), slice(8 * p, 8 * p + 8), slice(None))
        out_ref[at] = v if mix_out is None else out_ref[at] + v


def residual(b, u, sigma, beside_z, factor):
    comps, sx, sy, nz = u.shape
    half = comps // 2
    flat = u.reshape(comps * sx, sy, nz)
    row = iota(flat.shape, 1)
    near = jnp.where(row == 0, 0.0, roll(flat, 1, 1)) + jnp.where(row == sy - 1, 0.0, roll(flat, -1, 1))
    near = near.reshape(u.shape) + permute(flat.reshape(-1, nz), beside_z).reshape(u.shape)
    zero = jnp.zeros((comps, 1, sy, nz), f32)
    near = near + jnp.concatenate([zero, u[:, :-1]], axis=1) + jnp.concatenate([u[:, 1:], zero], axis=1)
    out = b - (6.0 * u - near) * factor
    turned = jnp.concatenate([sigma[None] * u[half:], -(sigma[None] * u[:half])], axis=0)
    return out + turned


def add_faces(r, faces_x, faces_y, factor):
    comps, sx, sy, nz = r.shape
    row = iota((comps * sx, sy, nz), 1)
    flat = r.reshape(comps * sx, sy, nz)
    flat = flat + jnp.where(row == 0, faces_y[0] * factor, 0.0) + jnp.where(row == sy - 1, faces_y[1] * factor, 0.0)
    r = flat.reshape(r.shape)
    low = r[:, :1] + faces_x[0][:, None] * factor
    high = r[:, sx - 1 :] + faces_x[1][:, None] * factor
    return jnp.concatenate([low, r[:, 1 : sx - 1], high], axis=1)


def restrict(u, t):
    comps, sx, sy, nz = u.shape
    v = u.reshape(comps * sx // 2, 2, sy, nz)
    v = pair_rows((v[:, 0] + v[:, 1]).reshape(-1, nz), t)
    v = (v + roll(v, nz // 2, 1)) * 0.125
    return v.reshape(comps, sx // 2, sy // 2, nz)


def kernel(
    axes, sizes, src_hbm, cls_hbm, cond_hbm, depth_hbm, inv_hbm, out,
    src, cls, cond, depth, inv, in_sem, block_in, block_out, w, w_row, b0, x0, r0, sig0, sig1, b1, x1, r1, d1, t,
    send_x, recv_x, send_y, recv_y, csend_x, crecv_x, csend_y, crecv_y, send_sem, recv_sem,
):
    comps, sx, sy, nz = src.shape
    named = ((src_hbm, src), (cls_hbm, cls), (cond_hbm, cond), (depth_hbm, depth), (inv_hbm, inv))
    loads = [pltpu.make_async_copy(a, b, in_sem.at[i]) for i, (a, b) in enumerate(named)]
    for load in loads:
        load.start()
    me = [lax.axis_index(a) for a in axes]
    has = [me[0] > 0, me[0] < sizes[0] - 1, me[1] > 0, me[1] < sizes[1] - 1]

    def device(d):
        n = sizes[d // 2]
        return {axes[d // 2]: lax.rem(me[d // 2] + (n - 1 if d % 2 == 0 else 1), n)}

    barrier = pltpu.get_barrier_semaphore()
    for d in range(4):
        @pl.when(has[d])
        def _(d=d):
            pl.semaphore_signal(barrier, inc=1, device_id=device(d), device_id_type=MESH)

        @pl.when(jnp.logical_not(has[d]))
        def _(d=d):
            for ref in [(recv_x, crecv_x), (recv_y, crecv_y)][d // 2]:
                if ref is recv_y:
                    ref[d % 2] = jnp.zeros(ref.shape[1:], f32)
                else:
                    for e in range(ref.shape[0]):
                        ref[e, d % 2] = jnp.zeros(ref.shape[2:], f32)

    def copy(e, d):
        if d < 2:
            s, r = (send_x.at[e - 3], recv_x.at[e - 3]) if e >= 3 else (csend_x.at[e], crecv_x.at[e])
        else:
            s, r = (send_y, recv_y) if e >= 3 else (csend_y.at[e], crecv_y.at[e])
        k = d % 2
        return pltpu.make_async_remote_copy(
            src_ref=s.at[k], dst_ref=r.at[1 - k], send_sem=send_sem.at[e, d], recv_sem=recv_sem.at[e, d ^ 1],
            device_id=device(d), device_id_type=MESH,
        )

    def launch(e, directions=range(4)):
        for d in directions:
            @pl.when(has[d])
            def _(d=d):
                copy(e, d).start()

    def start(e, u):
        c, ux, uy, _ = u.shape
        flat = u.reshape(c * ux, uy, nz)
        for k in range(2):
            csend_x[e, k] = pack(u[:, k * (ux - 1)])
        launch(e, (0, 1))
        for k in range(2):
            csend_y[e, k] = pack(flat[:, k * (uy - 1) : k * (uy - 1) + 1])
        launch(e, (2, 3))

    def faces(e):
        return [unpack(crecv_x[e, k]) for k in range(2)], [unpack(crecv_y[e, k]) for k in range(2)]

    def finish(e, directions=range(4)):
        for d in directions:
            @pl.when(has[d])
            def _(d=d):
                copy(e, d ^ 1).wait_recv()

    q = nz // 4
    def z_of(lane):
        zi = jnp.where(lane >= 2 * q, 1, 0)
        rest = lane - 2 * q * zi
        zic = jnp.where(rest >= q, 1, 0)
        return 4 * (rest - q * zic) + 2 * zic + zi
    to_lanes = jnp.where(iota((nz, nz), 0) == z_of(iota((nz, nz), 1)), 1.0, 0.0).astype(bf16)
    from_lanes = jnp.where(iota((nz, nz), 1) == z_of(iota((nz, nz), 0)), 1.0, 0.0).astype(bf16)

    beside0 = jnp.where(jnp.abs(z_of(iota((nz, nz), 0)) - z_of(iota((nz, nz), 1))) == 1, 1.0, 0.0).astype(bf16)
    def zc_of(lane):
        return z_of(lane - jnp.where(lane >= 2 * q, 2 * q, 0)) // 2
    near1 = jnp.abs(zc_of(iota((nz, nz), 0)) - zc_of(iota((nz, nz), 1))) == 1
    beside1 = jnp.where(near1 & (iota((nz, nz), 0) < 2 * q), 1.0, 0.0).astype(bf16)

    for i in (0, 3, 4):
        loads[i].wait()

    lane = iota((1, nz), 1)
    zb = zc_of(lane)
    ids0 = jnp.zeros((1, nz), jnp.int32)
    for k in range(depth.shape[0]):
        ids0 = jnp.where(zb == k, depth[k], ids0)
    ids1 = jnp.where(first_half((1, nz), q), ids0, roll(ids0, q, 1))

    layers, size, _ = inv.shape
    hi, lo = split(jnp.concatenate([inv[layer] for layer in range(layers)], axis=1))
    w[:size, :] = hi
    w[size:, :] = lo
    for k, part in enumerate((hi, lo, hi)):
        w_row[:, k * layers * size : (k + 1) * layers * size] = part

    def mix(a, b):
        side = jnp.where(b >= nz, 1, 0)
        lane = b - nz * side
        second = jnp.where(lane >= 2 * q, 1, 0)
        return jnp.where(a == nz * second + z_of(lane - 2 * q * second + 2 * q * side), 1.0, 0.0).astype(bf16)
    wide = (2 * nz, 2 * nz)
    mix_in, mix_out = mix(iota(wide, 0), iota(wide, 1)), mix(iota(wide, 1), iota(wide, 0))

    smooth(src[...], x0, w, w_row, ids0, nz // 2, damping, block_in, block_out, mix_in=mix_in)
    pl.semaphore_wait(barrier, sum(jnp.where(h, 1, 0) for h in has))
    flat = x0[...].reshape(comps * sx, sy, nz)
    for k in range(2):
        face = x0[:, k * (sx - 1)]
        face = pair_rows(face.reshape(comps * sy, nz), t).reshape(comps, sy // 2, nz)
        csend_x[0, k] = pack((face + roll(face, nz // 2, 2)) * 0.125)
    launch(0, (0, 1))
    for k in range(2):
        send_y[k] = flat[:, k * (sy - 1) : k * (sy - 1) + 1]
        face = send_y[k].reshape(comps * sx // 2, 2, 1, nz)
        face = face[:, 0] + face[:, 1]
        csend_y[0, k] = pack((face + roll(face, nz // 2, 2)) * 0.125)
    launch(0, (2, 3))

    loads[1].wait()
    kinds = dot(cls[...].reshape(-1, nz).astype(f32).astype(bf16), to_lanes)
    loads[2].wait()
    sigma = jnp.zeros_like(kinds)
    for k in range(cond.shape[0]):
        sigma = jnp.where(kinds == float(k), cond[k], sigma)
    sigma = sigma.reshape(sx, sy, nz)
    sig0[...] = sigma
    sig1[...] = restrict(sigma[None], t)[0]

    b0[...] = permute(src[...].reshape(-1, nz), to_lanes).reshape(src.shape)
    r0[...] = residual(b0[...], x0[...], sig0[...], beside0, 1.0)
    for k in range(2):
        for h in range(2):
            send_x[h, k] = x0[h * (comps // 2) : (h + 1) * (comps // 2), k * (sx - 1)]
    b1[...] = restrict(r0[...], t)
    finish(0)
    launch(3)
    b1[...] = add_faces(b1[...], *faces(0), 1.0)

    smooth(b1[...], x1, w, w_row, ids1, q, damping * 4.0, block_in, block_out)
    start(1, x1[...])
    r1[...] = residual(b1[...], x1[...], sig1[...], beside1, 0.25)
    finish(1)
    launch(4, (0, 1))
    smooth(add_faces(r1[...], *faces(1), 0.25), d1, w, w_row, ids1, q, damping * 4.0, block_in, block_out)
    xc = x1[...] + d1[...]
    start(2, xc)
    cx, cy = sx // 2, sy // 2
    spread = repeat_rows(xc.reshape(-1, nz), t).reshape(comps, cx, 1, sy, nz)
    spread = jnp.concatenate([spread, spread], axis=2).reshape(src.shape)
    x0[...] = x0[...] + spread
    r0[...] = residual(b0[...], x0[...], sig0[...], beside0, 1.0)
    out[...] = permute(x0[...].reshape(-1, nz), from_lanes).reshape(out.shape)
    finish(3)
    finish(4, (0, 1))
    finish(2)
    faces_x, faces_y = faces(2)
    for k in range(2):
        faces_x[k] = jnp.concatenate([recv_x[0, k], recv_x[1, k]], axis=0) + repeat_rows(faces_x[k].reshape(-1, nz), t).reshape(comps, sy, nz)
        face = faces_y[k].reshape(comps * cx, 1, 1, nz)
        faces_y[k] = recv_y[k] + jnp.concatenate([face, face], axis=1).reshape(comps * sx, 1, nz)
    smooth(
        add_faces(r0[...], faces_x, faces_y, 1.0), out, w, w_row, ids0, nz // 2, damping, block_in, block_out, mix_out=mix_out
    )
    for e in range(5):
        for d in range(4 if e < 4 else 2):
            @pl.when(has[d])
            def _(e=e, d=d):
                copy(e, d).wait_send()


def solution(mesh):
    axes = ("gx", "gy")
    sizes = tuple(mesh.shape[a] for a in axes)

    def per_device(source, cell_class, class_conductivity, layer_of_depth, inverses):
        operands = (source, cell_class, class_conductivity, layer_of_depth, inverses)
        comps, sx, sy, nz = source.shape
        layers, size, _ = inverses.shape
        cx, cy = sx // 2, sy // 2
        vmem = pl.BlockSpec(memory_space=pltpu.VMEM)
        hbm = pl.BlockSpec(memory_space=pltpu.HBM)
        fine, coarse = (comps, sx, sy, nz), (comps, cx, cy, nz)
        scratch = [
            ((sx // 4 * (sy // 8), size, nz), f32), ((sx // 4 * (sy // 8), size, nz), f32),
            ((2 * size, layers * size), bf16), ((size, 3 * layers * size), bf16), (fine, f32), (fine, f32), (fine, f32), ((sx, sy, nz), f32), ((cx, cy, nz), f32),
            (coarse, f32), (coarse, f32), (coarse, f32), (coarse, f32), ((comps * cx * sy, nz), f32),
        ]
        scratch += [((2, 2, comps // 2, sy, nz), f32)] * 2 + [((2, comps * sx, 1, nz), f32)] * 2
        scratch += [((3, 2, comps // 2, cy, nz), f32)] * 2 + [((3, 2, comps * cx // 2, 1, nz), f32)] * 2
        return pl.pallas_call(
            functools.partial(kernel, axes, sizes),
            out_shape=jax.ShapeDtypeStruct(source.shape, f32),
            in_specs=[hbm] * 5,
            out_specs=vmem,
            scratch_shapes=[pltpu.VMEM(source.shape, f32), pltpu.VMEM(cell_class.shape, jnp.int32)]
            + [pltpu.SMEM(class_conductivity.shape, f32), pltpu.SMEM(layer_of_depth.shape, jnp.int32)]
            + [pltpu.VMEM(inverses.shape, f32), pltpu.SemaphoreType.DMA((5,))]
            + [pltpu.VMEM(s, t) for s, t in scratch]
            + [pltpu.SemaphoreType.DMA((5, 4)), pltpu.SemaphoreType.DMA((5, 4))],
            compiler_params=pltpu.CompilerParams(
                collective_id=0, has_side_effects=True, vmem_limit_bytes=50 * 2**20
            ),
        )(*(pltpu.with_memory_space_constraint(v, pltpu.HBM) for v in operands))

    return jax.shard_map(
        per_device,
        mesh=mesh,
        in_specs=(P(None, "gx", "gy", None), P("gx", "gy", None), P(), P(), P()),
        out_specs=P(None, "gx", "gy", None),
        check_vma=False,
    )
```
